128 devices in a mesh: row: 16 (over x, y_lo, core), col: 8 (over y_hi, z).
Axes of the slice: x: 4, y: 4 (y_hi: 2, y_lo: 2; y = y_hi * 2 + y_lo), z: 4, core: 2. Of those that a mesh axis runs over, the one named last changes fastest.
Arguments:
- front_init: float32 [16384, 16384], P('row', 'col'), as said below
- child_tiles: bfloat16 [4096, 256, 256], P(('row', 'col'))
- child_dest: int32 [4096], P(('row', 'col')), may hold values from 0 to 4095, as said below
Outputs:
- panel_factor: float32 [16384, 1024], P('row')
- schur_update: float32 [16384, 16384], P('row', 'col')
The draws below stay inside these ranges and needn't reach their ends.
Inputs may be any that keep to these rules, and one draw needn't show every extreme that they name: `child_dest`: t = 64 * tile row + tile column. A tile held at col index c has its tile column in c * 8 to (c + 1) * 8 - 1. Of one device's tiles at most 4 have tile rows in one block of 4 tile rows, and in every column of the mesh one such block gets exactly 4 from every device of that column. The leading 1024 x 1024 block of front_init plus any child tiles added to it is strictly diagonally dominant.
All inputs are finite; a program needn't handle non-finite values.
Results may differ from the reference program's by a relative error of at most 0.0003.
Values may be sent and summed in bfloat16 or wider, within the bound.
A program may use at most 192 MiB of HBM per device.

```python
import jax
import jax.numpy as jnp
from jax import lax

NF = 16384
PW = 1024
TW = 256
CAP = 4
CTD = 32
NT = 64
TRD = 4
TCD = 8
NCHILD = 4096


def route_tiles(key):
    base_key = jax.random.fold_in(key, 11)
    row_count = NF // (TRD * TW)
    col_count = NF // (TCD * TW)
    device_count = row_count * col_count
    hot_key, perm_key, order_key, row_key, col_key = jax.random.split(base_key, 5)
    hot_rows = jax.random.randint(hot_key, (col_count,), 0, row_count)
    device_col = jnp.arange(device_count) % col_count
    hot_device = hot_rows[device_col]
    other_slots = (row_count - 1) * CAP
    perm_keys = jax.random.split(perm_key, device_count)
    perms = jax.vmap(lambda sub_key: jax.random.permutation(sub_key, other_slots))(perm_keys)
    picked = perms[:, :CTD - CAP] // CAP
    picked = picked + (picked >= hot_device[:, None]).astype(jnp.int32)
    hot_block = jnp.broadcast_to(hot_device[:, None], (device_count, CAP))
    owners = jnp.concatenate([hot_block, picked], axis=1).astype(jnp.int32)
    order_keys = jax.random.split(order_key, device_count)
    shuffle = jax.vmap(lambda sub_key: jax.random.permutation(sub_key, CTD))(order_keys)
    owners = jnp.take_along_axis(owners, shuffle, axis=1)
    tile_row = owners * TRD + jax.random.randint(row_key, (device_count, CTD), 0, TRD)
    tile_col = device_col[:, None] * TCD + jax.random.randint(col_key, (device_count, CTD), 0, TCD)
    return (tile_row * NT + tile_col).reshape(-1).astype(jnp.int32)


def draw_child_dest(key, part):
    return route_tiles(key)


def draw_child_tiles(key, part):
    targets = route_tiles(key)
    pivot_tiles = PW // TW
    target_row = targets // NT
    target_col = targets % NT
    in_pivot = (target_row < pivot_tiles) & (target_col < pivot_tiles)
    pivot_ids = jnp.arange(pivot_tiles, dtype=jnp.int32)
    row_match = target_row[:, None] == pivot_ids[None, :]
    col_match = target_col[:, None] == pivot_ids[None, :]
    row_hits = jnp.sum((row_match & in_pivot[:, None]).astype(jnp.int32), axis=0)
    col_hits = jnp.sum((col_match & in_pivot[:, None]).astype(jnp.int32), axis=0)
    row_crowd = jnp.sum(jnp.where(row_match, row_hits[None, :], 0), axis=1)
    col_crowd = jnp.sum(jnp.where(col_match, col_hits[None, :], 0), axis=1)
    crowding = jnp.maximum(jnp.maximum(row_crowd, col_crowd), 1).astype(jnp.float32)
    values = jax.random.uniform(jax.random.fold_in(key, 5), (NCHILD, TW, TW), jnp.float32, -0.5, 0.5)
    tile_scale = jax.random.uniform(jax.random.fold_in(key, 7), (NCHILD,), jnp.float32, 0.2, 1.0)
    positive = (values + 0.5) * tile_scale[:, None, None]
    chosen = jnp.where(in_pivot[:, None, None], positive, values)
    factor = jnp.where(in_pivot, 0.5 / (TW * crowding), 1.0).astype(jnp.float32)
    return (chosen * factor[:, None, None]).astype(jnp.bfloat16)


def draw_front_init(key, part):
    unit = jax.random.uniform(jax.random.fold_in(key, 3), (NF, NF), jnp.float32)
    signed = 2.0 * unit - 1.0
    row_ids = jax.lax.broadcasted_iota(jnp.int32, (NF, NF), 0)
    col_ids = jax.lax.broadcasted_iota(jnp.int32, (NF, NF), 1)
    amplitude = 2.42 * PW ** (-0.25)
    root_width = PW ** 0.5
    diag_value = jnp.where(row_ids < PW, 2.6 + 2.6 * unit, root_width * (1.25 + 1.25 * unit))
    both_pivot = (row_ids < PW) & (col_ids < PW)
    either_pivot = (row_ids < PW) | (col_ids < PW)
    neighbour = jnp.abs(row_ids - col_ids) == 1
    pivot_off = jnp.where(neighbour, -(0.4 + 0.4 * unit), unit * (0.4 / PW))
    off_value = jnp.where(both_pivot, pivot_off, jnp.where(either_pivot, signed * amplitude, signed))
    return jnp.where(row_ids == col_ids, diag_value, off_value).astype(jnp.float32)


def setup_inputs(seed: int = 0) -> dict:
    key_of = jax.random.split(jax.random.key(seed), 4)
    front_init = draw_front_init(jax.random.fold_in(key_of[3], 71), 0)
    child_tiles = draw_child_tiles(jax.random.fold_in(key_of[3], 71), 0)
    child_dest = draw_child_dest(jax.random.fold_in(key_of[3], 71), 0)
    return {"front_init": front_init, "child_tiles": child_tiles, "child_dest": child_dest}


def reference(front_init, child_tiles, child_dest):
    tile_sums = jnp.zeros((NT * NT, TW, TW), jnp.float32).at[child_dest].add(child_tiles.astype(jnp.float32))
    added_tiles = tile_sums.reshape(NT, NT, TW, TW).transpose(0, 2, 1, 3).reshape(NF, NF)
    front_sum = front_init + added_tiles
    column_panel = front_sum[:, :PW]
    pivot_raw = column_panel[:PW]
    pivot_sym = (pivot_raw + pivot_raw.T) * 0.5
    pivot_factor = jnp.linalg.cholesky(pivot_sym)
    panel_factor = jax.scipy.linalg.solve_triangular(pivot_factor, column_panel.T, lower=True).T
    schur_update = front_sum - jnp.dot(panel_factor.astype(jnp.float32), panel_factor.T.astype(jnp.float32), precision=lax.Precision.HIGHEST, preferred_element_type=jnp.float32)
    return (panel_factor, schur_update)
```

```python
import jax
import jax.numpy as jnp
from jax import lax
from jax.experimental import pallas as pl
from jax.experimental.pallas import tpu as pltpu
from jax.sharding import PartitionSpec as P

PW = 1024
TW = 256
CAP = 4
NT = 64
ROWS = 16
COLS = 8
SLOTS = ROWS * CAP
MIB = 1024 * 1024
MESH = pl.DeviceIdType.MESH
ANY = pl.BlockSpec(memory_space=pl.ANY)

HI = lax.Precision.HIGHEST
NB = 128


def block_inverse(block):
    rows = lax.broadcasted_iota(jnp.int32, (NB, NB), 0)
    lanes = lax.broadcasted_iota(jnp.int32, (NB, NB), 1)
    left = block
    right = jnp.where(rows == lanes, 1.0, 0.0).astype(jnp.float32)
    done = []
    for group in range(NB // 8):
        height = NB - 8 * group
        row_ids = lax.broadcasted_iota(jnp.int32, (height, NB), 0)
        cols = [
            jnp.broadcast_to(left[:, 8 * group + j : 8 * group + j + 1], (height, NB))
            for j in range(8)
        ]
        scales = []
        for i in range(8):
            pivot = cols[i][i : i + 1, :]
            scales.append(lax.rsqrt(pivot))
            mult = jnp.where(row_ids > i, cols[i] * (1.0 / pivot), 0.0)
            left = left - mult * left[i : i + 1, :]
            right = right - mult * right[i : i + 1, :]
            for j in range(i + 1, 8):
                cols[j] = cols[j] - mult * cols[j][i : i + 1, :]
        done.append(right[:8] * jnp.concatenate(scales, axis=0))
        left = left[8:]
        right = right[8:]
    return jnp.concatenate(done, axis=0)


def dot_nt(a, b):
    return lax.dot_general(a, b, (((1,), (1,)), ((), ())), precision=HI, preferred_element_type=jnp.float32)


def dot_nn(a, b):
    return lax.dot_general(a, b, (((1,), (0,)), ((), ())), precision=HI, preferred_element_type=jnp.float32)


def chol_kernel(raw_ref, out_ref, a_ref, w_ref):
    n = raw_ref.shape[0]
    steps = n // NB
    step = pl.program_id(0)

    @pl.when(step == 0)
    def _():
        for i in range(steps):
            for k in range(i + 1):
                ri, rk = slice(i * NB, (i + 1) * NB), slice(k * NB, (k + 1) * NB)
                a_ref[ri, rk] = (raw_ref[ri, rk] + raw_ref[rk, ri].T) * 0.5
        w_ref[...] = jnp.zeros_like(w_ref)

    here = pl.ds(pl.multiple_of(step * NB, NB), NB)
    inv = block_inverse(a_ref[here, here])
    for j in range(steps):

        @pl.when(step == j)
        def _(j=j):
            me = slice(j * NB, (j + 1) * NB)
            w_ref[me, me] = inv
            if j > 0:
                below = dot_nn(a_ref[me, : j * NB], w_ref[: j * NB, : j * NB])
                w_ref[me, : j * NB] = -dot_nn(inv, below)
            if j + 1 < steps:
                rest = slice((j + 1) * NB, n)
                col = dot_nt(a_ref[rest, me], inv)
                a_ref[rest, me] = col
                for k in range(j + 1, steps):
                    low = col[(k - j - 1) * NB :]
                    a_ref[k * NB :, k * NB : (k + 1) * NB] -= dot_nt(low, low[:NB])
            else:
                out_ref[...] = w_ref[...]


def chol_inverse(raw):
    n = raw.shape[0]
    return pl.pallas_call(
        chol_kernel,
        grid=(n // NB,),
        out_shape=jax.ShapeDtypeStruct((n, n), jnp.float32),
        in_specs=[pl.BlockSpec((n, n), lambda i: (0, 0))],
        out_specs=pl.BlockSpec((n, n), lambda i: (0, 0)),
        scratch_shapes=[pltpu.VMEM((n, n), jnp.float32), pltpu.VMEM((n, n), jnp.float32)],
        compiler_params=pltpu.CompilerParams(vmem_limit_bytes=48 * 1024 * 1024),
        name="chol_inverse",
    )(raw)


def pack_kernel(dest_ref, tiles_ref, out_ref, target_ref, count_ref, sems):
    def clear_count(i, carry):
        count_ref[i] = 0
        return carry

    def clear_target(i, carry):
        target_ref[i] = -1
        return carry

    lax.fori_loop(0, ROWS, clear_count, 0)
    lax.fori_loop(0, SLOTS, clear_target, 0)
    count = tiles_ref.shape[0]

    def place(i, carry):
        tile = dest_ref[i]
        tile_row = tile >> 6
        owner = tile_row >> 2
        rank = count_ref[owner]
        count_ref[owner] = rank + 1
        slot = owner * CAP + rank
        target_ref[slot] = (tile_row & 3) * 8 + (tile & 7)
        pltpu.make_async_copy(tiles_ref.at[i], out_ref.at[slot], sems.at[i]).start()
        return carry

    def finish(i, carry):
        pltpu.make_async_copy(tiles_ref.at[i], out_ref.at[i], sems.at[i]).wait()
        return carry

    lax.fori_loop(0, count, place, 0)
    lax.fori_loop(0, count, finish, 0)


def pack(child_tiles, child_dest):
    count = child_tiles.shape[0]
    return pl.pallas_call(
        pack_kernel,
        out_shape=(
            jax.ShapeDtypeStruct((SLOTS, TW, TW), jnp.bfloat16),
            jax.ShapeDtypeStruct((SLOTS,), jnp.int32),
        ),
        in_specs=[pl.BlockSpec(memory_space=pltpu.SMEM), ANY],
        out_specs=(ANY, pl.BlockSpec(memory_space=pltpu.SMEM)),
        scratch_shapes=[pltpu.SMEM((ROWS,), jnp.int32), pltpu.SemaphoreType.DMA((count,))],
        name="pack",
    )(child_dest, child_tiles)


def build_lists(places_ref, head_ref, next_ref):
    def clear(i, carry):
        head_ref[i] = -1
        return carry

    lax.fori_loop(0, 32, clear, 0)

    def link(i, carry):
        slot = SLOTS - 1 - i
        tile = places_ref[slot]

        @pl.when(tile >= 0)
        def _():
            next_ref[slot] = head_ref[tile]
            head_ref[tile] = slot

        return carry

    lax.fori_loop(0, SLOTS, link, 0)


def add_children(tile, total_ref, arrived_ref, head_ref, next_ref):
    def more(slot):
        return slot >= 0

    def add(slot):
        total_ref[...] += arrived_ref[slot].astype(jnp.float32)
        return next_ref[slot]

    lax.while_loop(more, add, head_ref[tile])


def panel_kernel(places_ref, front_ref, arrived_ref, out_ref, head_ref, next_ref):
    step = pl.program_id(0)

    @pl.when(step == 0)
    def _():
        build_lists(places_ref, head_ref, next_ref)

    out_ref[...] = front_ref[...]
    add_children((step // 4) * 8 + step % 4, out_ref, arrived_ref, head_ref, next_ref)


def panel_sum(places, front_init, arrived):
    return pl.pallas_call(
        panel_kernel,
        grid=(16,),
        out_shape=jax.ShapeDtypeStruct((front_init.shape[0], PW), jnp.float32),
        in_specs=[
            pl.BlockSpec(memory_space=pltpu.SMEM),
            pl.BlockSpec((TW, TW), lambda i: (i // 4, i % 4)),
            pl.BlockSpec((SLOTS, TW, TW), lambda i: (0, 0, 0), pipeline_mode=pl.Buffered(1)),
        ],
        out_specs=pl.BlockSpec((TW, TW), lambda i: (i // 4, i % 4)),
        scratch_shapes=[pltpu.SMEM((32,), jnp.int32), pltpu.SMEM((SLOTS,), jnp.int32)],
        compiler_params=pltpu.CompilerParams(vmem_limit_bytes=24 * MIB),
        name="panel_sum",
    )(places, front_init, arrived)


def spread_kernel(
    p_ref, w_ref, prs_ref, wa_ref,
    s_pr1, r_pr1, s_ps1, r_ps1, s_w1, r_w1, s_pr2, r_pr2, s_pr3, r_pr3,
    s_ps2, r_ps2, s_ps3, r_ps3, s_w2, r_w2, s_w3, r_w3, s_w4, r_w4, local,
):
    r = lax.axis_index("row")
    c = lax.axis_index("col")
    m, k = r // 2, r % 2
    yh, z = c // 4, c % 4
    root = (r == 0) & (c == 0)

    def remote(src, dst, send, recv, dev):
        return pltpu.make_async_remote_copy(src, dst, send, recv, device_id=dev, device_id_type=MESH)

    def rows(start, size):
        return pl.ds(pl.multiple_of(start, 8), size)

    def pr1(i):
        return remote(p_ref.at[rows(128 * i, 128)], prs_ref.at[rows(128 * i, 128)], s_pr1.at[i], r_pr1.at[0], (r, i))

    def ps1(i):
        rho = k * 8 + i
        return remote(
            p_ref.at[rows(128 * i, 128)], prs_ref.at[rows(PW + 128 * rho, 128)], s_ps1.at[i], r_ps1.at[0], (rho, m)
        )

    def w1(q):
        return remote(w_ref.at[rows(8 * q, 8)], wa_ref.at[rows(8 * q, 8)], s_w1.at[q], r_w1.at[0], (q // 8, q % 8))

    own_pr = pltpu.make_async_copy(p_ref.at[pl.ds(0, 128)], prs_ref.at[pl.ds(0, 128)], local.at[0])
    own_ps = pltpu.make_async_copy(p_ref.at[pl.ds(0, 128)], prs_ref.at[pl.ds(PW, 128)], local.at[1])
    own_w = pltpu.make_async_copy(w_ref.at[pl.ds(0, 8)], wa_ref.at[pl.ds(0, 8)], local.at[2])

    def each(lo, hi, fn):
        def step(i, carry):
            fn(i)
            return carry

        lax.fori_loop(lo, hi, step, 0)

    @pl.when(c == 0)
    def _():
        own_pr.start()

        @pl.when(r == 0)
        def _():
            own_ps.start()
            own_w.start()
            each(1, ROWS * COLS, lambda q: w1(q).start())

        @pl.when(r > 0)
        def _():
            ps1(0).start()

        ps1(4).start()
        for i in range(1, 8):
            pr1(i).start()
            if i != 4:
                ps1(i).start()

    pair = (r, lax.rem(c + 4, 8))
    other_core = (2 * m + 1 - k, c)
    mine = rows(128 * c, 128)
    theirs = rows(128 * lax.rem(c + 4, 8), 128)

    def pr2():
        return remote(prs_ref.at[mine], prs_ref.at[mine], s_pr2.at[0], r_pr2.at[0], pair)

    def pr3(dz, which):
        part = (mine, theirs)[which]
        i = (dz - 1) * 2 + which
        return remote(
            prs_ref.at[part], prs_ref.at[part], s_pr3.at[i], r_pr3.at[i], (r, yh * 4 + lax.rem(z + dz, 4))
        )

    def ps_rows(o):
        return rows(PW + 128 * (2 * lax.rem(m + 8 - o, 8) + k), 128)

    def ps2(o):
        part = ps_rows(0)
        return remote(prs_ref.at[part], prs_ref.at[part], s_ps2.at[o], r_ps2.at[o], (2 * lax.rem(m + o, 8) + k, c))

    def ps3(o):
        part = ps_rows(o)
        return remote(prs_ref.at[part], prs_ref.at[part], s_ps3.at[o], r_ps3.at[o], other_core)

    def w2(o):
        part = rows(8 * (r * 8 + c), 8)
        return remote(wa_ref.at[part], wa_ref.at[part], s_w2.at[o], r_w2.at[o], (r, lax.rem(c + o, 8)))

    def w_rows(o):
        return rows(64 * (2 * lax.rem(m + 8 - o, 8) + k), 64)

    def w3(o):
        part = w_rows(0)
        return remote(wa_ref.at[part], wa_ref.at[part], s_w3.at[o], r_w3.at[o], (2 * lax.rem(m + o, 8) + k, c))

    def w4(o):
        part = w_rows(o)
        return remote(wa_ref.at[part], wa_ref.at[part], s_w4.at[o], r_w4.at[o], other_core)

    @pl.when(c > 0)
    def _():
        pr1(0).wait_recv()

    @pl.when(c == 0)
    def _():
        own_pr.wait()

    pr2().start()

    @pl.when(root)
    def _():
        own_w.wait()
        own_ps.wait()

    @pl.when(jnp.logical_not(root))
    def _():
        w1(0).wait_recv()

    each(1, 8, lambda o: w2(o).start())

    @pl.when(jnp.logical_not(root))
    def _():
        ps1(0).wait_recv()

    each(1, 8, lambda o: ps2(o).start())
    ps3(0).start()
    for dz in (1, 3, 2):
        pr3(dz, 0).start()
    pr2().wait_recv()
    for dz in (1, 3, 2):
        pr3(dz, 1).start()
    each(1, 8, lambda o: w2(o).wait_recv())
    each(1, 8, lambda o: w3(o).start())
    w4(0).start()

    def forward_w(o):
        w3(o).wait_recv()
        w4(o).start()

    each(1, 8, forward_w)

    def forward_ps(o):
        ps2(o).wait_recv()
        ps3(o).start()

    each(1, 8, forward_ps)

    @pl.when(c == 0)
    def _():
        @pl.when(r == 0)
        def _():
            each(1, ROWS * COLS, lambda q: w1(q).wait_send())

        @pl.when(r > 0)
        def _():
            ps1(0).wait_send()

        for i in range(1, 8):
            pr1(i).wait_send()
            ps1(i).wait_send()

    pr2().wait_send()
    for dz in (1, 2, 3):
        for which in (0, 1):
            pr3(dz, which).wait()

    def finish(o):
        w2(o).wait_send()
        w3(o).wait_send()
        ps2(o).wait_send()

    each(1, 8, finish)

    def finish_core(o):
        ps3(o).wait()
        w4(o).wait()

    each(0, 8, finish_core)


def spread(panel, inverse):
    dma = pltpu.SemaphoreType.DMA
    sizes = [8, 1, 8, 1, 128, 1, 1, 1, 6, 6, 8, 8, 8, 8, 8, 8, 8, 8, 8, 8, 3]
    return pl.pallas_call(
        spread_kernel,
        out_shape=(
            jax.ShapeDtypeStruct((3 * PW, PW), jnp.float32),
            jax.ShapeDtypeStruct((PW, PW), jnp.float32),
        ),
        in_specs=[ANY, ANY],
        out_specs=(ANY, ANY),
        scratch_shapes=[dma((size,)) for size in sizes],
        compiler_params=pltpu.CompilerParams(has_side_effects=True),
        name="spread",
    )(panel, inverse)


def split(x):
    high = x.astype(jnp.bfloat16)
    return high, (x - high.astype(jnp.float32)).astype(jnp.bfloat16)


def dot3(ah, al, bh, bl):
    def nt(a, b):
        return lax.dot_general(a, b, (((1,), (1,)), ((), ())), preferred_element_type=jnp.float32)

    return nt(ah, bh) + (nt(ah, bl) + nt(al, bh))


def update_kernel(
    places_ref, w_ref, prs_ref, front_ref, arrived_ref, factor_ref, schur_ref,
    wh_ref, wl_ref, fh_ref, fl_ref, head_ref, next_ref,
):
    step = pl.program_id(0)

    @pl.when(step == 0)
    def _():
        build_lists(places_ref, head_ref, next_ref)
        wh_ref[...], wl_ref[...] = split(w_ref[...])

    @pl.when(step < 12)
    def _():
        ah, al = split(prs_ref[...])
        here = pl.ds(pl.multiple_of(step * TW, TW), TW)
        for j in range(PW // TW):
            out = slice(j * TW, (j + 1) * TW)
            deep = slice(0, (j + 1) * TW)
            block = dot3(ah[:, deep], al[:, deep], wh_ref[out, deep], wl_ref[out, deep])
            fh_ref[here, out], fl_ref[here, out] = split(block)

            @pl.when(step < 4)
            def _():
                factor_ref[:, out] = block

    @pl.when(step >= 12)
    def _():
        tile = step - 12
        left = pl.ds(pl.multiple_of((tile // 8) * TW, TW), TW)
        right = pl.ds(pl.multiple_of(PW + (tile % 8) * TW, TW), TW)
        schur_ref[...] = front_ref[...] - dot3(fh_ref[left, :], fl_ref[left, :], fh_ref[right, :], fl_ref[right, :])
        add_children(tile, schur_ref, arrived_ref, head_ref, next_ref)


def update(places, inverse, strips, front_init, arrived):
    def tile_map(i):
        t = jnp.maximum(i - 12, 0)
        return (t // 8, t % 8)

    return pl.pallas_call(
        update_kernel,
        grid=(44,),
        out_shape=(
            jax.ShapeDtypeStruct((PW, PW), jnp.float32),
            jax.ShapeDtypeStruct(front_init.shape, jnp.float32),
        ),
        in_specs=[
            pl.BlockSpec(memory_space=pltpu.SMEM),
            pl.BlockSpec((PW, PW), lambda i: (0, 0), pipeline_mode=pl.Buffered(1)),
            pl.BlockSpec((TW, PW), lambda i: (jnp.minimum(i, 11), 0)),
            pl.BlockSpec((TW, TW), tile_map),
            pl.BlockSpec((SLOTS, TW, TW), lambda i: (0, 0, 0), pipeline_mode=pl.Buffered(1)),
        ],
        out_specs=(
            pl.BlockSpec((TW, PW), lambda i: (jnp.minimum(i, 3), 0)),
            pl.BlockSpec((TW, TW), tile_map),
        ),
        scratch_shapes=[
            pltpu.VMEM((PW, PW), jnp.bfloat16),
            pltpu.VMEM((PW, PW), jnp.bfloat16),
            pltpu.VMEM((3 * PW, PW), jnp.bfloat16),
            pltpu.VMEM((3 * PW, PW), jnp.bfloat16),
            pltpu.SMEM((32,), jnp.int32),
            pltpu.SMEM((SLOTS,), jnp.int32),
        ],
        compiler_params=pltpu.CompilerParams(vmem_limit_bytes=52 * MIB),
        name="update",
    )(places, inverse, strips, front_init, arrived)


def body(front_init, child_tiles, child_dest):
    outgoing, targets = pack(child_tiles, child_dest)
    arrived = lax.all_to_all(outgoing, "row", split_axis=0, concat_axis=0, tiled=True)
    places = lax.all_to_all(targets, "row", split_axis=0, concat_axis=0, tiled=True)
    panel = panel_sum(places, front_init, arrived)
    inverse = chol_inverse(panel)
    strips, inverse_all = spread(panel, inverse)
    return update(places, inverse_all, strips, front_init, arrived)


def solution(mesh):
    return jax.shard_map(
        body,
        mesh=mesh,
        in_specs=(P("row", "col"), P(("row", "col"), None, None), P(("row", "col"))),
        out_specs=(P("row", None), P("row", "col")),
        check_vma=False,
    )
```

```python
import jax
import jax.numpy as jnp
from jax import lax
from jax.experimental import pallas as pl
from jax.experimental.pallas import tpu as pltpu
from jax.sharding import PartitionSpec as P

PW = 1024
TW = 256
CAP = 4
NT = 64
ROWS = 16
COLS = 8
SLOTS = ROWS * CAP
MIB = 1024 * 1024
MESH = pl.DeviceIdType.MESH
ANY = pl.BlockSpec(memory_space=pl.ANY)

HI = lax.Precision.HIGHEST
NB = 128


def block_inverse(block):
    rows = lax.broadcasted_iota(jnp.int32, (NB, NB), 0)
    lanes = lax.broadcasted_iota(jnp.int32, (NB, NB), 1)
    left = block
    right = jnp.where(rows == lanes, 1.0, 0.0).astype(jnp.float32)
    done = []
    for group in range(NB // 8):
        height = NB - 8 * group
        row_ids = lax.broadcasted_iota(jnp.int32, (height, NB), 0)
        cols = [
            jnp.broadcast_to(left[:, 8 * group + j : 8 * group + j + 1], (height, NB))
            for j in range(8)
        ]
        scales = []
        for i in range(8):
            pivot = cols[i][i : i + 1, :]
            scales.append(lax.rsqrt(pivot))
            mult = jnp.where(row_ids > i, cols[i] * (1.0 / pivot), 0.0)
            left = left - mult * left[i : i + 1, :]
            right = right - mult * right[i : i + 1, :]
            for j in range(i + 1, 8):
                cols[j] = cols[j] - mult * cols[j][i : i + 1, :]
        done.append(right[:8] * jnp.concatenate(scales, axis=0))
        left = left[8:]
        right = right[8:]
    return jnp.concatenate(done, axis=0)


def dot_nt(a, b):
    return lax.dot_general(a, b, (((1,), (1,)), ((), ())), precision=HI, preferred_element_type=jnp.float32)


def dot_nn(a, b):
    return lax.dot_general(a, b, (((1,), (0,)), ((), ())), precision=HI, preferred_element_type=jnp.float32)


def symmetrise(raw_ref, a_ref):
    for i in range(PW // NB):
        for k in range(i + 1):
            ri, rk = slice(i * NB, (i + 1) * NB), slice(k * NB, (k + 1) * NB)
            a_ref[ri, rk] = (raw_ref[ri, rk] + raw_ref[rk, ri].T) * 0.5


def chol_inverse(a_ref, w_ref):
    n = a_ref.shape[0]
    steps = n // NB
    w_ref[...] = jnp.zeros_like(w_ref)

    def run(step, carry):
        here = pl.ds(pl.multiple_of(step * NB, NB), NB)
        inv = block_inverse(a_ref[here, here])
        for j in range(steps):

            @pl.when(step == j)
            def _(j=j):
                me = slice(j * NB, (j + 1) * NB)
                w_ref[me, me] = inv
                if j > 0:
                    below = dot_nn(a_ref[me, : j * NB], w_ref[: j * NB, : j * NB])
                    w_ref[me, : j * NB] = -dot_nn(inv, below)
                if j + 1 < steps:
                    rest = slice((j + 1) * NB, n)
                    col = dot_nt(a_ref[rest, me], inv)
                    a_ref[rest, me] = col
                    for k in range(j + 1, steps):
                        low = col[(k - j - 1) * NB :]
                        a_ref[k * NB :, k * NB : (k + 1) * NB] -= dot_nt(low, low[:NB])

        return carry

    lax.fori_loop(0, steps, run, 0)


def pack_kernel(dest_ref, tiles_ref, out_ref, target_ref, count_ref, sems):
    def clear_count(i, carry):
        count_ref[i] = 0
        return carry

    def clear_target(i, carry):
        target_ref[i] = -1
        return carry

    lax.fori_loop(0, ROWS, clear_count, 0)
    lax.fori_loop(0, SLOTS, clear_target, 0)
    count = tiles_ref.shape[0]

    def place(i, carry):
        tile = dest_ref[i]
        tile_row = tile >> 6
        owner = tile_row >> 2
        rank = count_ref[owner]
        count_ref[owner] = rank + 1
        slot = owner * CAP + rank
        target_ref[slot] = (tile_row & 3) * 8 + (tile & 7)
        pltpu.make_async_copy(tiles_ref.at[i], out_ref.at[slot], sems.at[i]).start()
        return carry

    def finish(i, carry):
        pltpu.make_async_copy(tiles_ref.at[i], out_ref.at[i], sems.at[i]).wait()
        return carry

    lax.fori_loop(0, count, place, 0)
    lax.fori_loop(0, count, finish, 0)


def pack(child_tiles, child_dest):
    count = child_tiles.shape[0]
    return pl.pallas_call(
        pack_kernel,
        out_shape=(
            jax.ShapeDtypeStruct((SLOTS, TW, TW), jnp.bfloat16),
            jax.ShapeDtypeStruct((SLOTS,), jnp.int32),
        ),
        in_specs=[pl.BlockSpec(memory_space=pltpu.SMEM), pl.BlockSpec(memory_space=pltpu.VMEM)],
        out_specs=(ANY, pl.BlockSpec(memory_space=pltpu.SMEM)),
        scratch_shapes=[pltpu.SMEM((ROWS,), jnp.int32), pltpu.SemaphoreType.DMA((count,))],
        compiler_params=pltpu.CompilerParams(vmem_limit_bytes=16 * MIB),
        name="pack",
    )(child_dest, child_tiles)


def build_lists(places_ref, head_ref, next_ref):
    def clear(i, carry):
        head_ref[i] = -1
        return carry

    lax.fori_loop(0, 32, clear, 0)

    def link(i, carry):
        slot = SLOTS - 1 - i
        tile = places_ref[slot]

        @pl.when(tile >= 0)
        def _():
            next_ref[slot] = head_ref[tile]
            head_ref[tile] = slot

        return carry

    lax.fori_loop(0, SLOTS, link, 0)


def add_children(tile, total_ref, arrived_ref, head_ref, next_ref):
    def more(slot):
        return slot >= 0

    def add(slot):
        total_ref[...] += arrived_ref[slot].astype(jnp.float32)
        return next_ref[slot]

    lax.while_loop(more, add, head_ref[tile])


def panel_kernel(places_ref, front_ref, arrived_ref, out_ref, head_ref, next_ref):
    step = pl.program_id(0)

    @pl.when(step == 0)
    def _():
        build_lists(places_ref, head_ref, next_ref)

    out_ref[...] = front_ref[...]
    add_children((step // 4) * 8 + step % 4, out_ref, arrived_ref, head_ref, next_ref)


def panel_sum(places, front_init, arrived):
    return pl.pallas_call(
        panel_kernel,
        grid=(16,),
        out_shape=jax.ShapeDtypeStruct((front_init.shape[0], PW), jnp.float32),
        in_specs=[
            pl.BlockSpec(memory_space=pltpu.SMEM),
            pl.BlockSpec((TW, TW), lambda i: (i // 4, i % 4)),
            pl.BlockSpec((SLOTS, TW, TW), lambda i: (0, 0, 0), pipeline_mode=pl.Buffered(1)),
        ],
        out_specs=pl.BlockSpec((TW, TW), lambda i: (i // 4, i % 4)),
        scratch_shapes=[pltpu.SMEM((32,), jnp.int32), pltpu.SMEM((SLOTS,), jnp.int32)],
        compiler_params=pltpu.CompilerParams(vmem_limit_bytes=24 * MIB),
        name="panel_sum",
    )(places, front_init, arrived)


def spread_kernel(
    p_ref, prs_ref, wa_ref, a_ref, w_ref, stage_ref,
    s_pr1, r_pr1, s_swap, r_swap, s_pr2, r_pr2, s_pr3, r_pr3, s_ps2, r_ps2, s_ps3, r_ps3,
    s_w1, r_w1, s_w2, r_w2, s_w3, r_w3, s_w4, r_w4, local,
):
    r = lax.axis_index("row")
    c = lax.axis_index("col")
    m, k = r // 2, r % 2
    yh, z = c // 4, c % 4
    root = (r == 0) & (c == 0)
    pair = (r, lax.rem(c + 4, 8))
    other_core = (2 * m + 1 - k, c)

    def remote(src, dst, send, recv, dev):
        return pltpu.make_async_remote_copy(src, dst, send, recv, device_id=dev, device_id_type=MESH)

    def rows(start, size):
        return pl.ds(pl.multiple_of(start, 8), size)

    def each(lo, hi, fn):
        def step(i, carry):
            fn(i)
            return carry

        lax.fori_loop(lo, hi, step, 0)

    mine = rows(128 * c, 128)
    theirs = rows(128 * lax.rem(c + 4, 8), 128)

    def pr1(i):
        part = rows(128 * i, 128)
        return remote(p_ref.at[part], prs_ref.at[part], s_pr1.at[i], r_pr1.at[0], (r, i))

    def pr2():
        return remote(prs_ref.at[mine], prs_ref.at[mine], s_pr2.at[0], r_pr2.at[0], pair)

    def pr3(dz, which):
        part = (mine, theirs)[which]
        i = (dz - 1) * 2 + which
        return remote(
            prs_ref.at[part], prs_ref.at[part], s_pr3.at[i], r_pr3.at[i], (r, yh * 4 + lax.rem(z + dz, 4))
        )

    def swap():
        there = rows(PW + PW * k + 128 * c, 128)
        return remote(prs_ref.at[mine], prs_ref.at[there], s_swap.at[0], r_swap.at[0], (2 * c + k, m))

    def ps_rows(o):
        return rows(PW + PW * k + 128 * lax.rem(m + 8 - o, 8), 128)

    def ps2(o):
        part = ps_rows(0)
        return remote(prs_ref.at[part], prs_ref.at[part], s_ps2.at[o], r_ps2.at[o], (2 * lax.rem(m + o, 8) + k, c))

    def ps3(o):
        part = ps_rows(o)
        return remote(prs_ref.at[part], prs_ref.at[part], s_ps3.at[o], r_ps3.at[o], other_core)

    def w1(q):
        part = rows(8 * q, 8)
        return remote(w_ref.at[part], wa_ref.at[part], s_w1.at[q], r_w1.at[0], (q // 8, q % 8))

    def w2(o):
        part = rows(8 * (r * 8 + c), 8)
        return remote(wa_ref.at[part], wa_ref.at[part], s_w2.at[o], r_w2.at[o], (r, lax.rem(c + o, 8)))

    def w_rows(o):
        return rows(64 * (2 * lax.rem(m + 8 - o, 8) + k), 64)

    def w3(o):
        part = w_rows(0)
        return remote(wa_ref.at[part], wa_ref.at[part], s_w3.at[o], r_w3.at[o], (2 * lax.rem(m + o, 8) + k, c))

    def w4(o):
        part = w_rows(o)
        return remote(wa_ref.at[part], wa_ref.at[part], s_w4.at[o], r_w4.at[o], other_core)

    def move(src, dst, sem):
        copy = pltpu.make_async_copy(src, dst, sem)
        copy.start()
        copy.wait()

    @pl.when(c == 0)
    def _():
        for i in (4, 2, 6, 1, 3, 5, 7):
            pr1(i).start()
        move(p_ref.at[pl.ds(0, 128)], stage_ref, local.at[0])
        move(stage_ref, prs_ref.at[pl.ds(0, 128)], local.at[1])

    @pl.when(c > 0)
    def _():
        pr1(0).wait_recv()

    pr2().start()

    @pl.when(m == c)
    def _():
        move(prs_ref.at[mine], stage_ref, local.at[0])
        move(stage_ref, prs_ref.at[ps_rows(0)], local.at[1])

    @pl.when(m != c)
    def _():
        swap().start()

    for dz in (2, 1, 3):
        pr3(dz, 0).start()

    @pl.when(m != c)
    def _():
        swap().wait_recv()

    each(1, 8, lambda o: ps2(o).start())
    ps3(0).start()

    @pl.when(root)
    def _():
        move(p_ref, w_ref, local.at[2])
        symmetrise(w_ref, a_ref)
        chol_inverse(a_ref, w_ref)
        each(1, ROWS * COLS, lambda q: w1(q).start())
        move(w_ref.at[pl.ds(0, 8)], wa_ref.at[pl.ds(0, 8)], local.at[2])

    pr2().wait_recv()
    for dz in (2, 1, 3):
        pr3(dz, 1).start()

    @pl.when(jnp.logical_not(root))
    def _():
        w1(0).wait_recv()

    each(1, 8, lambda o: w2(o).start())
    each(1, 8, lambda o: w2(o).wait_recv())
    each(1, 8, lambda o: w3(o).start())
    w4(0).start()

    def forward_ps(o):
        ps2(o).wait_recv()
        ps3(o).start()

    each(1, 8, forward_ps)

    def forward_w(o):
        w3(o).wait_recv()
        w4(o).start()

    each(1, 8, forward_w)

    @pl.when(root)
    def _():
        each(1, ROWS * COLS, lambda q: w1(q).wait_send())

    @pl.when(c == 0)
    def _():
        each(1, 8, lambda i: pr1(i).wait_send())

    @pl.when(m != c)
    def _():
        swap().wait_send()

    pr2().wait_send()
    for dz in (1, 2, 3):
        for which in (0, 1):
            pr3(dz, which).wait()

    def finish(o):
        w2(o).wait_send()
        w3(o).wait_send()
        ps2(o).wait_send()

    each(1, 8, finish)

    def finish_core(o):
        ps3(o).wait()
        w4(o).wait()

    each(0, 8, finish_core)


def spread(panel):
    dma = pltpu.SemaphoreType.DMA
    sizes = [8, 1, 1, 1, 1, 1, 6, 6, 8, 8, 8, 8, 128, 1, 8, 8, 8, 8, 8, 8, 3]
    return pl.pallas_call(
        spread_kernel,
        out_shape=(
            jax.ShapeDtypeStruct((3 * PW, PW), jnp.float32),
            jax.ShapeDtypeStruct((PW, PW), jnp.float32),
        ),
        in_specs=[ANY],
        out_specs=(ANY, ANY),
        scratch_shapes=[
            pltpu.VMEM((PW, PW), jnp.float32),
            pltpu.VMEM((PW, PW), jnp.float32),
            pltpu.VMEM((128, PW), jnp.float32),
        ]
        + [dma((size,)) for size in sizes],
        compiler_params=pltpu.CompilerParams(has_side_effects=True, vmem_limit_bytes=40 * MIB),
        name="spread",
    )(panel)


def split(x):
    high = x.astype(jnp.bfloat16)
    return high, (x - high.astype(jnp.float32)).astype(jnp.bfloat16)


def dot3(ah, al, bh, bl):
    def nt(a, b):
        return lax.dot_general(a, b, (((1,), (1,)), ((), ())), preferred_element_type=jnp.float32)

    return nt(ah, bh) + (nt(ah, bl) + nt(al, bh))


CHUNK = 512
FILL = 3 * PW // CHUNK


def update_kernel(
    places_ref, w_ref, prs_ref, front_ref, arrived_ref, factor_ref, schur_ref,
    wh_ref, wl_ref, fh_ref, fl_ref, head_ref, next_ref,
):
    step = pl.program_id(0)

    @pl.when(step == 0)
    def _():
        build_lists(places_ref, head_ref, next_ref)
        wh_ref[...], wl_ref[...] = split(w_ref[...])

    @pl.when(step < FILL)
    def _():
        ah, al = split(prs_ref[...])
        here = pl.ds(pl.multiple_of(step * CHUNK, CHUNK), CHUNK)
        for j in range(PW // TW):
            out = slice(j * TW, (j + 1) * TW)
            deep = slice(0, (j + 1) * TW)
            block = dot3(ah[:, deep], al[:, deep], wh_ref[out, deep], wl_ref[out, deep])
            fh_ref[here, out], fl_ref[here, out] = split(block)

            @pl.when(step < PW // CHUNK)
            def _():
                factor_ref[:, out] = block

    @pl.when(step >= FILL)
    def _():
        column = step - FILL
        right = pl.ds(pl.multiple_of(PW + column * TW, TW), TW)
        schur_ref[...] = front_ref[...] - dot3(fh_ref[:PW, :], fl_ref[:PW, :], fh_ref[right, :], fl_ref[right, :])
        for i in range(PW // TW):
            total = schur_ref.at[i * TW : (i + 1) * TW, :]
            add_children(i * 8 + column, total, arrived_ref, head_ref, next_ref)


def update(places, inverse, strips, front_init, arrived):
    def column_map(i):
        return (0, jnp.maximum(i - FILL, 0))

    return pl.pallas_call(
        update_kernel,
        grid=(FILL + 8,),
        out_shape=(
            jax.ShapeDtypeStruct((PW, PW), jnp.float32),
            jax.ShapeDtypeStruct(front_init.shape, jnp.float32),
        ),
        in_specs=[
            pl.BlockSpec(memory_space=pltpu.SMEM),
            pl.BlockSpec((PW, PW), lambda i: (0, 0), pipeline_mode=pl.Buffered(1)),
            pl.BlockSpec((CHUNK, PW), lambda i: (jnp.minimum(i, FILL - 1), 0)),
            pl.BlockSpec((PW, TW), column_map),
            pl.BlockSpec((SLOTS, TW, TW), lambda i: (0, 0, 0), pipeline_mode=pl.Buffered(1)),
        ],
        out_specs=(
            pl.BlockSpec((CHUNK, PW), lambda i: (jnp.minimum(i, PW // CHUNK - 1), 0)),
            pl.BlockSpec((PW, TW), column_map),
        ),
        scratch_shapes=[
            pltpu.VMEM((PW, PW), jnp.bfloat16),
            pltpu.VMEM((PW, PW), jnp.bfloat16),
            pltpu.VMEM((3 * PW, PW), jnp.bfloat16),
            pltpu.VMEM((3 * PW, PW), jnp.bfloat16),
            pltpu.SMEM((32,), jnp.int32),
            pltpu.SMEM((SLOTS,), jnp.int32),
        ],
        compiler_params=pltpu.CompilerParams(vmem_limit_bytes=58 * MIB),
        name="update",
    )(places, inverse, strips, front_init, arrived)


def body(front_init, child_tiles, child_dest):
    outgoing, targets = pack(child_tiles, child_dest)
    arrived = lax.all_to_all(outgoing, "row", split_axis=0, concat_axis=0, tiled=True)
    places = lax.all_to_all(targets, "row", split_axis=0, concat_axis=0, tiled=True)
    panel = panel_sum(places, front_init, arrived)
    strips, inverse = spread(panel)
    return update(places, inverse, strips, front_init, arrived)


def solution(mesh):
    return jax.shard_map(
        body,
        mesh=mesh,
        in_specs=(P("row", "col"), P(("row", "col"), None, None), P(("row", "col"))),
        out_specs=(P("row", None), P("row", "col")),
        check_vma=False,
    )
```

```python
import jax
import jax.numpy as jnp
from jax import lax
from jax.experimental import pallas as pl
from jax.experimental.pallas import tpu as pltpu
from jax.sharding import PartitionSpec as P

PW = 1024
TW = 256
CAP = 4
NT = 64
ROWS = 16
COLS = 8
SLOTS = ROWS * CAP
MIB = 1024 * 1024
MESH = pl.DeviceIdType.MESH
ANY = pl.BlockSpec(memory_space=pl.ANY)

HI = lax.Precision.HIGHEST
NB = 128


def block_inverse(block):
    rows = lax.broadcasted_iota(jnp.int32, (NB, NB), 0)
    lanes = lax.broadcasted_iota(jnp.int32, (NB, NB), 1)
    left = block
    right = jnp.where(rows == lanes, 1.0, 0.0).astype(jnp.float32)
    done = []
    for group in range(NB // 8):
        height = NB - 8 * group
        row_ids = lax.broadcasted_iota(jnp.int32, (height, NB), 0)
        cols = [
            jnp.broadcast_to(left[:, 8 * group + j : 8 * group + j + 1], (height, NB))
            for j in range(8)
        ]
        scales = []
        for i in range(8):
            pivot = cols[i][i : i + 1, :]
            scales.append(lax.rsqrt(pivot))
            mult = jnp.where(row_ids > i, cols[i] * (1.0 / pivot), 0.0)
            left = left - mult * left[i : i + 1, :]
            right = right - mult * right[i : i + 1, :]
            for j in range(i + 1, 8):
                cols[j] = cols[j] - mult * cols[j][i : i + 1, :]
        done.append(right[:8] * jnp.concatenate(scales, axis=0))
        left = left[8:]
        right = right[8:]
    return jnp.concatenate(done, axis=0)


def dot_nt(a, b):
    return lax.dot_general(a, b, (((1,), (1,)), ((), ())), precision=HI, preferred_element_type=jnp.float32)


def dot_nn(a, b):
    return lax.dot_general(a, b, (((1,), (0,)), ((), ())), precision=HI, preferred_element_type=jnp.float32)


def symmetrise(raw_ref, a_ref):
    for i in range(PW // NB):
        for k in range(i + 1):
            ri, rk = slice(i * NB, (i + 1) * NB), slice(k * NB, (k + 1) * NB)
            a_ref[ri, rk] = (raw_ref[ri, rk] + raw_ref[rk, ri].T) * 0.5


def chol_inverse(a_ref, w_ref, block_done):
    n = a_ref.shape[0]
    steps = n // NB
    w_ref[...] = jnp.zeros_like(w_ref)

    def run(step, carry):
        here = pl.ds(pl.multiple_of(step * NB, NB), NB)
        inv = block_inverse(a_ref[here, here])
        for j in range(steps):

            @pl.when(step == j)
            def _(j=j):
                me = slice(j * NB, (j + 1) * NB)
                w_ref[me, me] = inv
                if j > 0:
                    below = dot_nn(a_ref[me, : j * NB], w_ref[: j * NB, : j * NB])
                    w_ref[me, : j * NB] = -dot_nn(inv, below)
                if j + 1 < steps:
                    rest = slice((j + 1) * NB, n)
                    col = dot_nt(a_ref[rest, me], inv)
                    a_ref[rest, me] = col
                    for k in range(j + 1, steps):
                        low = col[(k - j - 1) * NB :]
                        a_ref[k * NB :, k * NB : (k + 1) * NB] -= dot_nt(low, low[:NB])

        block_done(step)
        return carry

    lax.fori_loop(0, steps, run, 0)


def pack_kernel(dest_ref, tiles_ref, out_ref, target_ref, count_ref, sems):
    def clear_count(i, carry):
        count_ref[i] = 0
        return carry

    def clear_target(i, carry):
        target_ref[i] = -1
        return carry

    lax.fori_loop(0, ROWS, clear_count, 0)
    lax.fori_loop(0, SLOTS, clear_target, 0)
    count = tiles_ref.shape[0]

    def place(i, carry):
        tile = dest_ref[i]
        tile_row = tile >> 6
        owner = tile_row >> 2
        rank = count_ref[owner]
        count_ref[owner] = rank + 1
        slot = owner * CAP + rank
        target_ref[slot] = (tile_row & 3) * 8 + (tile & 7)
        pltpu.make_async_copy(tiles_ref.at[i], out_ref.at[slot], sems.at[i]).start()
        return carry

    def finish(i, carry):
        pltpu.make_async_copy(tiles_ref.at[i], out_ref.at[i], sems.at[i]).wait()
        return carry

    lax.fori_loop(0, count, place, 0)
    lax.fori_loop(0, count, finish, 0)


def pack(child_tiles, child_dest):
    count = child_tiles.shape[0]
    return pl.pallas_call(
        pack_kernel,
        out_shape=(
            jax.ShapeDtypeStruct((SLOTS, TW, TW), jnp.bfloat16),
            jax.ShapeDtypeStruct((SLOTS,), jnp.int32),
        ),
        in_specs=[pl.BlockSpec(memory_space=pltpu.SMEM), pl.BlockSpec(memory_space=pltpu.VMEM)],
        out_specs=(ANY, pl.BlockSpec(memory_space=pltpu.SMEM)),
        scratch_shapes=[pltpu.SMEM((ROWS,), jnp.int32), pltpu.SemaphoreType.DMA((count,))],
        compiler_params=pltpu.CompilerParams(vmem_limit_bytes=16 * MIB),
        name="pack",
    )(child_dest, child_tiles)


PEERS = (
    (2, 1, 0), (2, 1, 1), (1, 1, 0), (1, 1, 1), (2, 0, 0), (2, 0, 1), (3, 1, 0), (3, 1, 1),
    (0, 1, 0), (0, 1, 1), (1, 0, 0), (1, 0, 1), (3, 0, 0), (3, 0, 1), (0, 0, 1),
)


def exchange_kernel(out_ref, target_ref, in_ref, place_ref, send, recv, target_send, target_recv, local):
    r = lax.axis_index("row")
    c = lax.axis_index("col")
    x, y, k = r // 4, (r // 2) % 2, r % 2
    here = pl.ds(r * CAP, CAP)
    copies = []
    for i, (dx, dy, dk) in enumerate(PEERS):
        peer = lax.rem(x + dx, 4) * 4 + lax.rem(y + dy, 2) * 2 + lax.rem(k + dk, 2)
        copies.append(
            pltpu.make_async_remote_copy(
                target_ref.at[peer], place_ref.at[r], target_send.at[i], target_recv.at[i],
                device_id=(peer, c), device_id_type=MESH,
            )
        )
        copies.append(
            pltpu.make_async_remote_copy(
                out_ref.at[pl.ds(peer * CAP, CAP)], in_ref.at[here], send.at[i], recv.at[i],
                device_id=(peer, c), device_id_type=MESH,
            )
        )
    copies.append(pltpu.make_async_copy(out_ref.at[here], in_ref.at[here], local.at[0]))
    copies.append(pltpu.make_async_copy(target_ref.at[r], place_ref.at[r], local.at[1]))
    for copy in copies:
        copy.start()
    for copy in copies:
        copy.wait()


def exchange(outgoing, targets):
    dma = pltpu.SemaphoreType.DMA
    padded = jnp.pad(targets.reshape(ROWS, 1, CAP), ((0, 0), (0, 7), (0, 128 - CAP)))
    arrived, places = pl.pallas_call(
        exchange_kernel,
        out_shape=(
            jax.ShapeDtypeStruct(outgoing.shape, outgoing.dtype),
            jax.ShapeDtypeStruct(padded.shape, padded.dtype),
        ),
        in_specs=[ANY, ANY],
        out_specs=(ANY, ANY),
        scratch_shapes=[dma((15,)), dma((15,)), dma((15,)), dma((15,)), dma((2,))],
        compiler_params=pltpu.CompilerParams(has_side_effects=True),
        name="exchange",
    )(outgoing, padded)
    return arrived, places[:, 0, :CAP].reshape(SLOTS)


def build_lists(places_ref, head_ref, next_ref):
    def clear(i, carry):
        head_ref[i] = -1
        return carry

    lax.fori_loop(0, 32, clear, 0)

    def link(i, carry):
        slot = SLOTS - 1 - i
        tile = places_ref[slot]

        @pl.when(tile >= 0)
        def _():
            next_ref[slot] = head_ref[tile]
            head_ref[tile] = slot

        return carry

    lax.fori_loop(0, SLOTS, link, 0)


def add_children(tile, total_ref, arrived_ref, head_ref, next_ref):
    def more(slot):
        return slot >= 0

    def add(slot):
        total_ref[...] += arrived_ref[slot].astype(jnp.float32)
        return next_ref[slot]

    lax.while_loop(more, add, head_ref[tile])


def panel_kernel(places_ref, front_ref, arrived_ref, out_ref, head_ref, next_ref):
    step = pl.program_id(0)

    @pl.when(step == 0)
    def _():
        build_lists(places_ref, head_ref, next_ref)

    out_ref[...] = front_ref[...]
    add_children((step // 4) * 8 + step % 4, out_ref, arrived_ref, head_ref, next_ref)


def panel_sum(places, front_init, arrived):
    return pl.pallas_call(
        panel_kernel,
        grid=(16,),
        out_shape=jax.ShapeDtypeStruct((front_init.shape[0], PW), jnp.float32),
        in_specs=[
            pl.BlockSpec(memory_space=pltpu.SMEM),
            pl.BlockSpec((TW, TW), lambda i: (i // 4, i % 4)),
            pl.BlockSpec((SLOTS, TW, TW), lambda i: (0, 0, 0), pipeline_mode=pl.Buffered(1)),
        ],
        out_specs=pl.BlockSpec((TW, TW), lambda i: (i // 4, i % 4)),
        scratch_shapes=[pltpu.SMEM((32,), jnp.int32), pltpu.SMEM((SLOTS,), jnp.int32)],
        compiler_params=pltpu.CompilerParams(vmem_limit_bytes=24 * MIB),
        name="panel_sum",
    )(places, front_init, arrived)


PARTS = 8
SUB = 128 // PARTS
CHIPS = ((2, 1), (1, 1), (3, 1), (2, 0), (0, 1), (1, 0), (3, 0))


def spread_kernel(
    p_ref, prs_ref, wa_ref, a_ref, w_ref, stage_ref,
    s_pr1, r_pr1, s_swap, r_swap, s_pry, r_pry, s_pr3, r_pr3, s_ps2, r_ps2, s_ps3, r_ps3,
    s_w1, r_w1, s_w2, r_w2, s_w3, r_w3, s_w4, r_w4, local,
):
    r = lax.axis_index("row")
    c = lax.axis_index("col")
    m, k = r // 2, r % 2
    x, y = m // 2, m % 2
    yh, z = c // 4, c % 4
    root = (r == 0) & (c == 0)
    other_core = (2 * m + 1 - k, c)

    def remote(src, dst, send, recv, dev):
        return pltpu.make_async_remote_copy(src, dst, send, recv, device_id=dev, device_id_type=MESH)

    def rows(start, size):
        return pl.ds(pl.multiple_of(start, 8), size)

    def each(lo, hi, fn):
        def step(i, carry):
            fn(i)
            return carry

        lax.fori_loop(lo, hi, step, 0)

    to_m = [m] + [lax.rem(x + dx, 4) * 2 + lax.rem(y + dy, 2) for dx, dy in CHIPS]
    from_m = [m] + [lax.rem(x + 4 - dx, 4) * 2 + lax.rem(y + dy, 2) for dx, dy in CHIPS]

    def piece_at(position):
        px, py = position // 2, position % 2
        turn = lax.rem(px + 4 - c // 2, 4)
        return (turn // 2) * 4 + lax.rem(turn, 2) * 2 + lax.rem(py + 2 - c % 2, 2)

    def part_of(piece, ch):
        return rows(128 * piece + SUB * ch, SUB)

    def pr1(ch, i, half):
        part = part_of(i + 4 * half, ch)
        j = (ch * 4 + i) * 2 + half
        return remote(p_ref.at[part], prs_ref.at[part], s_pr1.at[j], r_pr1.at[ch * 2 + half], (r, i))

    def pry(ch, half):
        part = part_of(z + 4 * half, ch)
        j = ch * 2 + half
        return remote(prs_ref.at[part], prs_ref.at[part], s_pry.at[j], r_pry.at[j], (r, z + 4))

    def pr3(ch, dz, half):
        part = part_of(z + 4 * half, ch)
        i = ch * 6 + (dz - 1) * 2 + half
        return remote(
            prs_ref.at[part], prs_ref.at[part], s_pr3.at[i], r_pr3.at[i], (r, yh * 4 + lax.rem(z + dz, 4))
        )

    def swap(ch):
        there = rows(PW + PW * k + 128 * c + SUB * ch, SUB)
        spot = lax.rem(yh * 2 + z // 2 + x, 4) * 2 + lax.rem(z + y, 2)
        return remote(prs_ref.at[part_of(c, ch)], prs_ref.at[there], s_swap.at[ch], r_swap.at[ch], (2 * spot + k, m))

    def ps_rows(ch, o):
        return rows(PW + PW * k + 128 * piece_at(from_m[o]) + SUB * ch, SUB)

    def ps2(ch, o):
        part = ps_rows(ch, 0)
        i = ch * 8 + o
        return remote(prs_ref.at[part], prs_ref.at[part], s_ps2.at[i], r_ps2.at[i], (2 * to_m[o] + k, c))

    def ps3(ch, o):
        part = ps_rows(ch, o)
        i = ch * 8 + o
        return remote(prs_ref.at[part], prs_ref.at[part], s_ps3.at[i], r_ps3.at[i], other_core)

    def w1(q):
        part = rows(8 * q, 8)
        return remote(w_ref.at[part], wa_ref.at[part], s_w1.at[q], r_w1.at[0], (q // 8, q % 8))

    def w2(o):
        part = rows(8 * (r * 8 + c), 8)
        return remote(wa_ref.at[part], wa_ref.at[part], s_w2.at[o], r_w2.at[o], (r, lax.rem(c + o, 8)))

    def w_rows(o):
        return rows(64 * (2 * from_m[o] + k), 64)

    def w3(o):
        part = w_rows(0)
        return remote(wa_ref.at[part], wa_ref.at[part], s_w3.at[o], r_w3.at[o], (2 * to_m[o] + k, c))

    def w4(o):
        part = w_rows(o)
        return remote(wa_ref.at[part], wa_ref.at[part], s_w4.at[o], r_w4.at[o], other_core)

    def move(src, dst, sem):
        copy = pltpu.make_async_copy(src, dst, sem)
        copy.start()
        copy.wait()

    stays = (m == 0) & (c == 0)

    def send_parts(ch):
        for i in (2, 1, 3):
            for half in (0, 1):
                pr1(ch, i, half).start()

    @pl.when(c == 0)
    def _():
        send_parts(0)
        loads = [
            pltpu.make_async_copy(p_ref.at[pl.ds(512 * h, 128)], stage_ref.at[pl.ds(128 * h, 128)], local.at[h])
            for h in (0, 1)
        ]
        for copy in loads:
            copy.start()
        for copy in loads:
            copy.wait()
        stores = [
            pltpu.make_async_copy(stage_ref.at[pl.ds(128 * h, 128)], prs_ref.at[pl.ds(512 * h, 128)], local.at[h])
            for h in (0, 1)
        ]
        for copy in stores:
            copy.start()

        @pl.when(m == 0)
        def _():
            move(stage_ref.at[pl.ds(0, 128)], prs_ref.at[rows(PW + PW * k, 128)], local.at[2])

        for copy in stores:
            copy.wait()

    def take(ch):
        @pl.when((c == 0) & (ch > 0))
        def _():
            send_parts(ch)

        @pl.when((yh == 0) & (z > 0))
        def _():
            for half in (0, 1):
                pr1(ch, 0, half).wait_recv()

        @pl.when(yh == 0)
        def _():
            for half in (1, 0):
                pry(ch, half).start()

        @pl.when(yh == 1)
        def _():
            for half in (1, 0):
                pry(ch, half).wait_recv()

        @pl.when(jnp.logical_not(stays))
        def _():
            swap(ch).start()

        for dz in (2, 1, 3):
            for half in (0, 1):
                pr3(ch, dz, half).start()

    def fan(ch):
        @pl.when(jnp.logical_not(stays))
        def _():
            swap(ch).wait_recv()

        for o in range(1, 8):
            ps2(ch, o).start()
        ps3(ch, 0).start()

    def pipeline(i):
        @pl.when(i < PARTS)
        def _():
            take(i)

        @pl.when(i > 0)
        def _():
            fan(i - 1)

    each(0, PARTS + 1, pipeline)

    def send_block(step):
        def send(i):
            q = step * 16 + i

            @pl.when(q > 0)
            def _():
                w1(q).start()

        each(0, 16, send)

    @pl.when(root)
    def _():
        move(p_ref, w_ref, local.at[2])
        symmetrise(w_ref, a_ref)
        chol_inverse(a_ref, w_ref, send_block)
        move(w_ref.at[pl.ds(0, 8)], wa_ref.at[pl.ds(0, 8)], local.at[2])

    def cross(ch):
        for o in range(1, 8):
            ps2(ch, o).wait_recv()
            ps3(ch, o).start()

    @pl.when(jnp.logical_not(root))
    def _():
        w1(0).wait_recv()

    each(1, 8, lambda o: w2(o).start())
    each(1, 8, lambda o: w2(o).wait_recv())
    for o in range(1, 8):
        w3(o).start()
    w4(0).start()
    each(0, PARTS, cross)
    for o in range(1, 8):
        w3(o).wait_recv()
        w4(o).start()

    @pl.when(root)
    def _():
        each(1, ROWS * COLS, lambda q: w1(q).wait_send())

    def finish(ch):
        @pl.when(c == 0)
        def _():
            for i in (1, 2, 3):
                for half in (0, 1):
                    pr1(ch, i, half).wait_send()

        @pl.when(yh == 0)
        def _():
            for half in (0, 1):
                pry(ch, half).wait_send()

        @pl.when(jnp.logical_not(stays))
        def _():
            swap(ch).wait_send()

        for dz in (1, 2, 3):
            for half in (0, 1):
                pr3(ch, dz, half).wait()
        for o in range(1, 8):
            ps2(ch, o).wait_send()
        for o in range(8):
            ps3(ch, o).wait()

    each(0, PARTS, finish)
    for o in range(1, 8):
        w2(o).wait_send()
        w3(o).wait_send()
    for o in range(8):
        w4(o).wait()


def spread(panel):
    dma = pltpu.SemaphoreType.DMA
    n = PARTS
    sizes = [8 * n, 2 * n, n, n, 2 * n, 2 * n, 6 * n, 6 * n, 8 * n, 8 * n, 8 * n, 8 * n, 128, 1, 8, 8, 8, 8, 8, 8, 3]
    return pl.pallas_call(
        spread_kernel,
        out_shape=(
            jax.ShapeDtypeStruct((3 * PW, PW), jnp.float32),
            jax.ShapeDtypeStruct((PW, PW), jnp.float32),
        ),
        in_specs=[ANY],
        out_specs=(ANY, ANY),
        scratch_shapes=[
            pltpu.VMEM((PW, PW), jnp.float32),
            pltpu.VMEM((PW, PW), jnp.float32),
            pltpu.VMEM((256, PW), jnp.float32),
        ]
        + [dma((size,)) for size in sizes],
        compiler_params=pltpu.CompilerParams(has_side_effects=True, vmem_limit_bytes=40 * MIB),
        name="spread",
    )(panel)


def split(x):
    high = x.astype(jnp.bfloat16)
    return high, (x - high.astype(jnp.float32)).astype(jnp.bfloat16)


def dot3(ah, al, bh, bl):
    def nt(a, b):
        return lax.dot_general(a, b, (((1,), (1,)), ((), ())), preferred_element_type=jnp.float32)

    return nt(ah, bh) + (nt(ah, bl) + nt(al, bh))


CHUNK = 512
FILL = 3 * PW // CHUNK


def update_kernel(
    places_ref, w_ref, prs_ref, front_ref, arrived_ref, factor_ref, schur_ref,
    wh_ref, wl_ref, fh_ref, fl_ref, head_ref, next_ref,
):
    step = pl.program_id(0)

    @pl.when(step == 0)
    def _():
        build_lists(places_ref, head_ref, next_ref)
        wh_ref[...], wl_ref[...] = split(w_ref[...])

    @pl.when(step < FILL)
    def _():
        ah, al = split(prs_ref[...])
        here = pl.ds(pl.multiple_of(step * CHUNK, CHUNK), CHUNK)
        for j in range(PW // TW):
            out = slice(j * TW, (j + 1) * TW)
            deep = slice(0, (j + 1) * TW)
            block = dot3(ah[:, deep], al[:, deep], wh_ref[out, deep], wl_ref[out, deep])
            fh_ref[here, out], fl_ref[here, out] = split(block)

            @pl.when(step < PW // CHUNK)
            def _():
                factor_ref[:, out] = block

    @pl.when(step >= FILL)
    def _():
        column = step - FILL
        right = pl.ds(pl.multiple_of(PW + column * TW, TW), TW)
        schur_ref[...] = front_ref[...] - dot3(fh_ref[:PW, :], fl_ref[:PW, :], fh_ref[right, :], fl_ref[right, :])
        for i in range(PW // TW):
            total = schur_ref.at[i * TW : (i + 1) * TW, :]
            add_children(i * 8 + column, total, arrived_ref, head_ref, next_ref)


def update(places, inverse, strips, front_init, arrived):
    def column_map(i):
        return (0, jnp.maximum(i - FILL, 0))

    return pl.pallas_call(
        update_kernel,
        grid=(FILL + 8,),
        out_shape=(
            jax.ShapeDtypeStruct((PW, PW), jnp.float32),
            jax.ShapeDtypeStruct(front_init.shape, jnp.float32),
        ),
        in_specs=[
            pl.BlockSpec(memory_space=pltpu.SMEM),
            pl.BlockSpec((PW, PW), lambda i: (0, 0), pipeline_mode=pl.Buffered(1)),
            pl.BlockSpec((CHUNK, PW), lambda i: (jnp.minimum(i, FILL - 1), 0)),
            pl.BlockSpec((PW, TW), column_map),
            pl.BlockSpec((SLOTS, TW, TW), lambda i: (0, 0, 0), pipeline_mode=pl.Buffered(1)),
        ],
        out_specs=(
            pl.BlockSpec((CHUNK, PW), lambda i: (jnp.minimum(i, PW // CHUNK - 1), 0)),
            pl.BlockSpec((PW, TW), column_map),
        ),
        scratch_shapes=[
            pltpu.VMEM((PW, PW), jnp.bfloat16),
            pltpu.VMEM((PW, PW), jnp.bfloat16),
            pltpu.VMEM((3 * PW, PW), jnp.bfloat16),
            pltpu.VMEM((3 * PW, PW), jnp.bfloat16),
            pltpu.SMEM((32,), jnp.int32),
            pltpu.SMEM((SLOTS,), jnp.int32),
        ],
        compiler_params=pltpu.CompilerParams(vmem_limit_bytes=58 * MIB),
        name="update",
    )(places, inverse, strips, front_init, arrived)


def body(front_init, child_tiles, child_dest):
    outgoing, targets = pack(child_tiles, child_dest)
    arrived, places = exchange(outgoing, targets)
    panel = panel_sum(places, front_init, arrived)
    strips, inverse = spread(panel)
    return update(places, inverse, strips, front_init, arrived)


def solution(mesh):
    return jax.shard_map(
        body,
        mesh=mesh,
        in_specs=(P("row", "col"), P(("row", "col"), None, None), P(("row", "col"))),
        out_specs=(P("row", None), P("row", "col")),
        check_vma=False,
    )
```

```python
import jax
import jax.numpy as jnp
from jax import lax
from jax.experimental import pallas as pl
from jax.experimental.pallas import tpu as pltpu
from jax.sharding import PartitionSpec as P

PW = 1024
TW = 256
CAP = 4
NT = 64
ROWS = 16
COLS = 8
SLOTS = ROWS * CAP
MIB = 1024 * 1024
MESH = pl.DeviceIdType.MESH
ANY = pl.BlockSpec(memory_space=pl.ANY)

HI = lax.Precision.HIGHEST
NB = 128


def block_inverse(block):
    rows = lax.broadcasted_iota(jnp.int32, (NB, NB), 0)
    lanes = lax.broadcasted_iota(jnp.int32, (NB, NB), 1)
    left = block
    right = jnp.where(rows == lanes, 1.0, 0.0).astype(jnp.float32)
    done = []
    for group in range(NB // 8):
        height = NB - 8 * group
        row_ids = lax.broadcasted_iota(jnp.int32, (height, NB), 0)
        cols = [
            jnp.broadcast_to(left[:, 8 * group + j : 8 * group + j + 1], (height, NB))
            for j in range(8)
        ]
        scales = []
        for i in range(8):
            pivot = cols[i][i : i + 1, :]
            scales.append(lax.rsqrt(pivot))
            mult = jnp.where(row_ids > i, cols[i] * (1.0 / pivot), 0.0)
            left = left - mult * left[i : i + 1, :]
            right = right - mult * right[i : i + 1, :]
            for j in range(i + 1, 8):
                cols[j] = cols[j] - mult * cols[j][i : i + 1, :]
        done.append(right[:8] * jnp.concatenate(scales, axis=0))
        left = left[8:]
        right = right[8:]
    return jnp.concatenate(done, axis=0)


def dot_nt(a, b):
    return lax.dot_general(a, b, (((1,), (1,)), ((), ())), precision=HI, preferred_element_type=jnp.float32)


def dot_nn(a, b):
    return lax.dot_general(a, b, (((1,), (0,)), ((), ())), precision=HI, preferred_element_type=jnp.float32)


def symmetrise(raw_ref, a_ref):
    for i in range(PW // NB):
        for k in range(i + 1):
            ri, rk = slice(i * NB, (i + 1) * NB), slice(k * NB, (k + 1) * NB)
            a_ref[ri, rk] = (raw_ref[ri, rk] + raw_ref[rk, ri].T) * 0.5


def chol_inverse(a_ref, w_ref, block_done):
    n = a_ref.shape[0]
    steps = n // NB
    w_ref[...] = jnp.zeros_like(w_ref)

    def run(step, carry):
        here = pl.ds(pl.multiple_of(step * NB, NB), NB)
        inv = block_inverse(a_ref[here, here])
        for j in range(steps):

            @pl.when(step == j)
            def _(j=j):
                me = slice(j * NB, (j + 1) * NB)
                w_ref[me, me] = inv
                if j > 0:
                    below = dot_nn(a_ref[me, : j * NB], w_ref[: j * NB, : j * NB])
                    w_ref[me, : j * NB] = -dot_nn(inv, below)
                if j + 1 < steps:
                    rest = slice((j + 1) * NB, n)
                    col = dot_nt(a_ref[rest, me], inv)
                    a_ref[rest, me] = col
                    for k in range(j + 1, steps):
                        low = col[(k - j - 1) * NB :]
                        a_ref[k * NB :, k * NB : (k + 1) * NB] -= dot_nt(low, low[:NB])

        block_done(step)
        return carry

    lax.fori_loop(0, steps, run, 0)


def pack_kernel(dest_ref, tiles_ref, out_ref, target_ref, count_ref, sems):
    def clear_count(i, carry):
        count_ref[i] = 0
        return carry

    def clear_target(i, carry):
        target_ref[i] = -1
        return carry

    lax.fori_loop(0, ROWS, clear_count, 0)
    lax.fori_loop(0, SLOTS, clear_target, 0)
    count = tiles_ref.shape[0]

    def place(i, carry):
        tile = dest_ref[i]
        tile_row = tile >> 6
        owner = tile_row >> 2
        rank = count_ref[owner]
        count_ref[owner] = rank + 1
        slot = owner * CAP + rank
        target_ref[slot] = (tile_row & 3) * 8 + (tile & 7)
        pltpu.make_async_copy(tiles_ref.at[i], out_ref.at[slot], sems.at[i]).start()
        return carry

    def finish(i, carry):
        pltpu.make_async_copy(tiles_ref.at[i], out_ref.at[i], sems.at[i]).wait()
        return carry

    lax.fori_loop(0, count, place, 0)
    lax.fori_loop(0, count, finish, 0)


def pack(child_tiles, child_dest):
    count = child_tiles.shape[0]
    return pl.pallas_call(
        pack_kernel,
        out_shape=(
            jax.ShapeDtypeStruct((SLOTS, TW, TW), jnp.bfloat16),
            jax.ShapeDtypeStruct((SLOTS,), jnp.int32),
        ),
        in_specs=[pl.BlockSpec(memory_space=pltpu.SMEM), pl.BlockSpec(memory_space=pltpu.VMEM)],
        out_specs=(ANY, pl.BlockSpec(memory_space=pltpu.SMEM)),
        scratch_shapes=[pltpu.SMEM((ROWS,), jnp.int32), pltpu.SemaphoreType.DMA((count,))],
        compiler_params=pltpu.CompilerParams(vmem_limit_bytes=58 * MIB),
        name="pack",
    )(child_dest, child_tiles)


PEERS = (
    (2, 1, 0), (2, 1, 1), (1, 1, 0), (1, 1, 1), (2, 0, 0), (2, 0, 1), (3, 1, 0), (3, 1, 1),
    (0, 1, 0), (0, 1, 1), (1, 0, 0), (1, 0, 1), (3, 0, 0), (3, 0, 1), (0, 0, 1),
)


def exchange_kernel(out_ref, target_ref, in_ref, place_ref, send, recv, target_send, target_recv, local):
    r = lax.axis_index("row")
    c = lax.axis_index("col")
    x, y, k = r // 4, (r // 2) % 2, r % 2
    here = pl.ds(r * CAP, CAP)
    copies = []
    for i, (dx, dy, dk) in enumerate(PEERS):
        peer = lax.rem(x + dx, 4) * 4 + lax.rem(y + dy, 2) * 2 + lax.rem(k + dk, 2)
        copies.append(
            pltpu.make_async_remote_copy(
                target_ref.at[peer], place_ref.at[r], target_send.at[i], target_recv.at[i],
                device_id=(peer, c), device_id_type=MESH,
            )
        )
        copies.append(
            pltpu.make_async_remote_copy(
                out_ref.at[pl.ds(peer * CAP, CAP)], in_ref.at[here], send.at[i], recv.at[i],
                device_id=(peer, c), device_id_type=MESH,
            )
        )
    copies.append(pltpu.make_async_copy(out_ref.at[here], in_ref.at[here], local.at[0]))
    copies.append(pltpu.make_async_copy(target_ref.at[r], place_ref.at[r], local.at[1]))
    for copy in copies:
        copy.start()
    for copy in copies:
        copy.wait()


def exchange(outgoing, targets):
    dma = pltpu.SemaphoreType.DMA
    padded = jnp.pad(targets.reshape(ROWS, 1, CAP), ((0, 0), (0, 7), (0, 128 - CAP)))
    arrived, places = pl.pallas_call(
        exchange_kernel,
        out_shape=(
            jax.ShapeDtypeStruct(outgoing.shape, outgoing.dtype),
            jax.ShapeDtypeStruct(padded.shape, padded.dtype),
        ),
        in_specs=[ANY, ANY],
        out_specs=(ANY, ANY),
        scratch_shapes=[dma((15,)), dma((15,)), dma((15,)), dma((15,)), dma((2,))],
        compiler_params=pltpu.CompilerParams(has_side_effects=True),
        name="exchange",
    )(outgoing, padded)
    return arrived, places[:, 0, :CAP].reshape(SLOTS)


def build_lists(places_ref, head_ref, next_ref):
    def clear(i, carry):
        head_ref[i] = -1
        return carry

    lax.fori_loop(0, 32, clear, 0)

    def link(i, carry):
        slot = SLOTS - 1 - i
        tile = places_ref[slot]

        @pl.when(tile >= 0)
        def _():
            next_ref[slot] = head_ref[tile]
            head_ref[tile] = slot

        return carry

    lax.fori_loop(0, SLOTS, link, 0)


def add_children(tile, total_ref, arrived_ref, head_ref, next_ref):
    def more(slot):
        return slot >= 0

    def add(slot):
        total_ref[...] += arrived_ref[slot].astype(jnp.float32)
        return next_ref[slot]

    lax.while_loop(more, add, head_ref[tile])


def panel_kernel(places_ref, front_ref, arrived_ref, out_ref, head_ref, next_ref):
    step = pl.program_id(0)

    @pl.when(step == 0)
    def _():
        build_lists(places_ref, head_ref, next_ref)

    out_ref[...] = front_ref[...]
    add_children((step // 4) * 8 + step % 4, out_ref, arrived_ref, head_ref, next_ref)


def panel_sum(places, front_init, arrived):
    return pl.pallas_call(
        panel_kernel,
        grid=(16,),
        out_shape=jax.ShapeDtypeStruct((front_init.shape[0], PW), jnp.float32),
        in_specs=[
            pl.BlockSpec(memory_space=pltpu.SMEM),
            pl.BlockSpec((TW, TW), lambda i: (i // 4, i % 4)),
            pl.BlockSpec((SLOTS, TW, TW), lambda i: (0, 0, 0), pipeline_mode=pl.Buffered(1)),
        ],
        out_specs=pl.BlockSpec((TW, TW), lambda i: (i // 4, i % 4)),
        scratch_shapes=[pltpu.SMEM((32,), jnp.int32), pltpu.SMEM((SLOTS,), jnp.int32)],
        compiler_params=pltpu.CompilerParams(vmem_limit_bytes=58 * MIB),
        name="panel_sum",
    )(places, front_init, arrived)


PARTS = 8
LAG = 1
SUB = 128 // PARTS
UPWARD = (1, 5, 2, 0)
DOWNWARD = (3, 7, 6, 4)
CHIPS = ((2, 1), (1, 1), (3, 1), (2, 0), (0, 1), (1, 0), (3, 0))


def spread_kernel(
    p_ref, prs_ref, wa_ref, a_ref, w_ref,
    s_flow, r_flow, s_swap, r_swap, s_pry, r_pry, s_pr3, r_pr3, s_ps2, r_ps2, s_ps3, r_ps3,
    s_w1, r_w1, s_w2, r_w2, s_w3, r_w3, s_w4, r_w4, local,
):
    r = lax.axis_index("row")
    c = lax.axis_index("col")
    m, k = r // 2, r % 2
    x, y = m // 2, m % 2
    yh, z = c // 4, c % 4
    root = (r == 0) & (c == 0)
    other_core = (2 * m + 1 - k, c)

    def remote(src, dst, send, recv, dev):
        return pltpu.make_async_remote_copy(src, dst, send, recv, device_id=dev, device_id_type=MESH)

    def rows(start, size):
        return pl.ds(pl.multiple_of(start, 8), size)

    def each(lo, hi, fn):
        def step(i, carry):
            fn(i)
            return carry

        lax.fori_loop(lo, hi, step, 0)

    to_m = [m] + [lax.rem(x + dx, 4) * 2 + lax.rem(y + dy, 2) for dx, dy in CHIPS]
    from_m = [m] + [lax.rem(x + 4 - dx, 4) * 2 + lax.rem(y + dy, 2) for dx, dy in CHIPS]

    def piece_at(position):
        px, py = position // 2, position % 2
        turn = lax.rem(px + 4 - c // 2, 4)
        return (turn // 2) * 4 + lax.rem(turn, 2) * 2 + lax.rem(py + 2 - c % 2, 2)

    def part_of(piece, ch):
        return rows(128 * piece + SUB * ch, SUB)

    def flow(ch, piece, src):
        part = part_of(piece, ch)
        there = lax.rem(z + (1 if piece in UPWARD else 3), 4)
        i = ch * 8 + piece
        return remote(src.at[part], prs_ref.at[part], s_flow.at[i], r_flow.at[i], (r, there))

    def pry(ch, half):
        part = part_of(z + 4 * half, ch)
        j = ch * 2 + half
        return remote(prs_ref.at[part], prs_ref.at[part], s_pry.at[j], r_pry.at[j], (r, z + 4))

    def pr3(ch, dz, half):
        part = part_of(z + 4 * half, ch)
        i = ch * 6 + (dz - 1) * 2 + half
        return remote(
            prs_ref.at[part], prs_ref.at[part], s_pr3.at[i], r_pr3.at[i], (r, yh * 4 + lax.rem(z + dz, 4))
        )

    def swap(ch):
        there = rows(PW + PW * k + 128 * c + SUB * ch, SUB)
        spot = lax.rem(yh * 2 + z // 2 + x, 4) * 2 + lax.rem(z + y, 2)
        return remote(prs_ref.at[part_of(c, ch)], prs_ref.at[there], s_swap.at[ch], r_swap.at[ch], (2 * spot + k, m))

    def ps_rows(ch, o):
        return rows(PW + PW * k + 128 * piece_at(from_m[o]) + SUB * ch, SUB)

    def ps2(ch, o):
        part = ps_rows(ch, 0)
        i = ch * 8 + o
        return remote(prs_ref.at[part], prs_ref.at[part], s_ps2.at[i], r_ps2.at[i], (2 * to_m[o] + k, c))

    def ps3(ch, o):
        part = ps_rows(ch, o)
        i = ch * 8 + o
        return remote(prs_ref.at[part], prs_ref.at[part], s_ps3.at[i], r_ps3.at[i], other_core)

    def w1(q):
        part = rows(8 * q, 8)
        return remote(w_ref.at[part], wa_ref.at[part], s_w1.at[q], r_w1.at[0], (q // 8, q % 8))

    def w2(o):
        part = rows(8 * (r * 8 + c), 8)
        return remote(wa_ref.at[part], wa_ref.at[part], s_w2.at[o], r_w2.at[o], (r, lax.rem(c + o, 8)))

    def w_rows(o):
        return rows(64 * (2 * from_m[o] + k), 64)

    def w3(o):
        part = w_rows(0)
        return remote(wa_ref.at[part], wa_ref.at[part], s_w3.at[o], r_w3.at[o], (2 * to_m[o] + k, c))

    def w4(o):
        part = w_rows(o)
        return remote(wa_ref.at[part], wa_ref.at[part], s_w4.at[o], r_w4.at[o], other_core)

    def move(src, dst, sem):
        copy = pltpu.make_async_copy(src, dst, sem)
        copy.start()
        copy.wait()

    stays = (m == 0) & (c == 0)

    def send_parts(ch):
        for up, down in zip(UPWARD, DOWNWARD):
            flow(ch, up, p_ref).start()
            flow(ch, down, p_ref).start()

    @pl.when(c == 0)
    def _():
        send_parts(0)
        move(p_ref, w_ref, local.at[0])
        move(w_ref, prs_ref.at[pl.ds(0, PW)], local.at[1])

        @pl.when(m == 0)
        def _():
            move(w_ref.at[pl.ds(0, 128)], prs_ref.at[rows(PW + PW * k, 128)], local.at[2])

    rises = (yh == 0) & ((z == 1) | (z == 2))
    falls = (yh == 0) & ((z == 2) | (z == 3))

    def forward(ch, pieces):
        for piece in pieces:
            flow(ch, piece, prs_ref).wait_recv()
            flow(ch, piece, prs_ref).start()

    def take(ch):
        @pl.when((c == 0) & (ch > 0))
        def _():
            send_parts(ch)

        @pl.when(rises)
        def _():
            forward(ch, UPWARD)

        @pl.when(falls)
        def _():
            forward(ch, DOWNWARD)

        @pl.when(yh == 0)
        def _():
            for half in (1, 0):
                pry(ch, half).start()

        @pl.when(yh == 1)
        def _():
            for half in (1, 0):
                pry(ch, half).wait_recv()

        @pl.when(jnp.logical_not(stays))
        def _():
            swap(ch).start()

        @pl.when(yh == 1)
        def _():
            for dz in (2, 1, 3):
                for half in (0, 1):
                    pr3(ch, dz, half).start()

    def fan(ch):
        @pl.when(jnp.logical_not(stays))
        def _():
            swap(ch).wait_recv()

        for o in range(1, 8):
            ps2(ch, o).start()
        ps3(ch, 0).start()

    def pipeline(i):
        @pl.when(i < PARTS)
        def _():
            take(i)

        @pl.when(i >= LAG)
        def _():
            fan(i - LAG)

    each(0, PARTS, pipeline)

    def send_block(step):
        def send(i):
            q = step * 16 + i

            @pl.when(q > 0)
            def _():
                w1(q).start()

        each(0, 16, send)

    @pl.when(root)
    def _():
        symmetrise(w_ref, a_ref)
        chol_inverse(a_ref, w_ref, send_block)
        move(w_ref.at[pl.ds(0, 8)], wa_ref.at[pl.ds(0, 8)], local.at[2])

    @pl.when(jnp.logical_not(root))
    def _():
        w1(0).wait_recv()

    each(1, 8, lambda o: w2(o).start())
    each(1, 8, lambda o: w2(o).wait_recv())
    for o in range(1, 8):
        w3(o).start()
    w4(0).start()
    each(PARTS, PARTS + LAG, pipeline)

    def cross(ch):
        for o in range(1, 8):
            ps2(ch, o).wait_recv()
            ps3(ch, o).start()

    each(0, PARTS, cross)
    for o in range(1, 8):
        w3(o).wait_recv()
        w4(o).start()

    @pl.when(root)
    def _():
        each(1, ROWS * COLS, lambda q: w1(q).wait_send())

    def finish(ch):
        def settle(pieces, done):
            for piece in pieces:
                copy = flow(ch, piece, prs_ref)
                copy.wait_send() if done else copy.wait_recv()

        @pl.when(rises | (c == 0))
        def _():
            settle(UPWARD, True)

        @pl.when(falls | (c == 0))
        def _():
            settle(DOWNWARD, True)

        @pl.when((yh == 0) & (z == 1))
        def _():
            settle(DOWNWARD, False)

        @pl.when((yh == 0) & (z == 3))
        def _():
            settle(UPWARD, False)

        @pl.when(yh == 0)
        def _():
            for half in (0, 1):
                pry(ch, half).wait_send()

        @pl.when(jnp.logical_not(stays))
        def _():
            swap(ch).wait_send()

        @pl.when(yh == 1)
        def _():
            for dz in (1, 2, 3):
                for half in (0, 1):
                    pr3(ch, dz, half).wait()

        for o in range(1, 8):
            ps2(ch, o).wait_send()
        for o in range(8):
            ps3(ch, o).wait()

    each(0, PARTS, finish)
    for o in range(1, 8):
        w2(o).wait_send()
        w3(o).wait_send()
    for o in range(8):
        w4(o).wait()


def spread(panel):
    dma = pltpu.SemaphoreType.DMA
    n = PARTS
    sizes = [8 * n, 8 * n, n, n, 2 * n, 2 * n, 6 * n, 6 * n, 8 * n, 8 * n, 8 * n, 8 * n, 128, 1, 8, 8, 8, 8, 8, 8, 3]
    return pl.pallas_call(
        spread_kernel,
        out_shape=(
            jax.ShapeDtypeStruct((3 * PW, PW), jnp.float32),
            jax.ShapeDtypeStruct((PW, PW), jnp.float32),
        ),
        in_specs=[ANY],
        out_specs=(ANY, ANY),
        scratch_shapes=[
            pltpu.VMEM((PW, PW), jnp.float32),
            pltpu.VMEM((PW, PW), jnp.float32),
        ]
        + [dma((size,)) for size in sizes],
        compiler_params=pltpu.CompilerParams(has_side_effects=True, vmem_limit_bytes=58 * MIB),
        name="spread",
    )(panel)


def split(x):
    high = x.astype(jnp.bfloat16)
    return high, (x - high.astype(jnp.float32)).astype(jnp.bfloat16)


def dot3(ah, al, bh, bl):
    def nt(a, b):
        return lax.dot_general(a, b, (((1,), (1,)), ((), ())), preferred_element_type=jnp.float32)

    return nt(ah, bh) + (nt(ah, bl) + nt(al, bh))


CHUNK = 512
FILL = 3 * PW // CHUNK


def update_kernel(
    places_ref, w_ref, prs_ref, front_ref, arrived_ref, factor_ref, schur_ref,
    wh_ref, wl_ref, fh_ref, fl_ref, head_ref, next_ref,
):
    step = pl.program_id(0)

    @pl.when(step == 0)
    def _():
        build_lists(places_ref, head_ref, next_ref)
        wh_ref[...], wl_ref[...] = split(w_ref[...])

    @pl.when(step < FILL)
    def _():
        ah, al = split(prs_ref[...])
        here = pl.ds(pl.multiple_of(step * CHUNK, CHUNK), CHUNK)
        for j in range(PW // TW):
            out = slice(j * TW, (j + 1) * TW)
            deep = slice(0, (j + 1) * TW)
            block = dot3(ah[:, deep], al[:, deep], wh_ref[out, deep], wl_ref[out, deep])
            fh_ref[here, out], fl_ref[here, out] = split(block)

            @pl.when(step < PW // CHUNK)
            def _():
                factor_ref[:, out] = block

    @pl.when(step >= FILL)
    def _():
        column = step - FILL
        right = pl.ds(pl.multiple_of(PW + column * TW, TW), TW)
        schur_ref[...] = front_ref[...] - dot3(fh_ref[:PW, :], fl_ref[:PW, :], fh_ref[right, :], fl_ref[right, :])
        for i in range(PW // TW):
            total = schur_ref.at[i * TW : (i + 1) * TW, :]
            add_children(i * 8 + column, total, arrived_ref, head_ref, next_ref)


def update(places, inverse, strips, front_init, arrived):
    def column_map(i):
        return (0, jnp.maximum(i - FILL, 0))

    return pl.pallas_call(
        update_kernel,
        grid=(FILL + 8,),
        out_shape=(
            jax.ShapeDtypeStruct((PW, PW), jnp.float32),
            jax.ShapeDtypeStruct(front_init.shape, jnp.float32),
        ),
        in_specs=[
            pl.BlockSpec(memory_space=pltpu.SMEM),
            pl.BlockSpec((PW, PW), lambda i: (0, 0), pipeline_mode=pl.Buffered(1)),
            pl.BlockSpec((CHUNK, PW), lambda i: (jnp.minimum(i, FILL - 1), 0)),
            pl.BlockSpec((PW, TW), column_map),
            pl.BlockSpec((SLOTS, TW, TW), lambda i: (0, 0, 0), pipeline_mode=pl.Buffered(1)),
        ],
        out_specs=(
            pl.BlockSpec((CHUNK, PW), lambda i: (jnp.minimum(i, PW // CHUNK - 1), 0)),
            pl.BlockSpec((PW, TW), column_map),
        ),
        scratch_shapes=[
            pltpu.VMEM((PW, PW), jnp.bfloat16),
            pltpu.VMEM((PW, PW), jnp.bfloat16),
            pltpu.VMEM((3 * PW, PW), jnp.bfloat16),
            pltpu.VMEM((3 * PW, PW), jnp.bfloat16),
            pltpu.SMEM((32,), jnp.int32),
            pltpu.SMEM((SLOTS,), jnp.int32),
        ],
        compiler_params=pltpu.CompilerParams(vmem_limit_bytes=58 * MIB),
        name="update",
    )(places, inverse, strips, front_init, arrived)


def body(front_init, child_tiles, child_dest):
    outgoing, targets = pack(child_tiles, child_dest)
    arrived, places = exchange(outgoing, targets)
    panel = panel_sum(places, front_init, arrived)
    strips, inverse = spread(panel)
    return update(places, inverse, strips, front_init, arrived)


def solution(mesh):
    return jax.shard_map(
        body,
        mesh=mesh,
        in_specs=(P("row", "col"), P(("row", "col"), None, None), P(("row", "col"))),
        out_specs=(P("row", None), P("row", "col")),
        check_vma=False,
    )
```

```python
import jax
import jax.numpy as jnp
from jax import lax
from jax.experimental import pallas as pl
from jax.experimental.pallas import tpu as pltpu
from jax.sharding import PartitionSpec as P

PW = 1024
TW = 256
CAP = 4
NT = 64
ROWS = 16
COLS = 8
SLOTS = ROWS * CAP
MIB = 1024 * 1024
MESH = pl.DeviceIdType.MESH
ANY = pl.BlockSpec(memory_space=pl.ANY)

HI = lax.Precision.HIGHEST
NB = 128


def block_inverse(block):
    rows = lax.broadcasted_iota(jnp.int32, (NB, NB), 0)
    lanes = lax.broadcasted_iota(jnp.int32, (NB, NB), 1)
    left = block
    right = jnp.where(rows == lanes, 1.0, 0.0).astype(jnp.float32)
    done = []
    for group in range(NB // 8):
        height = NB - 8 * group
        row_ids = lax.broadcasted_iota(jnp.int32, (height, NB), 0)
        cols = [
            jnp.broadcast_to(left[:, 8 * group + j : 8 * group + j + 1], (height, NB))
            for j in range(8)
        ]
        scales = []
        for i in range(8):
            pivot = cols[i][i : i + 1, :]
            scales.append(lax.rsqrt(pivot))
            mult = jnp.where(row_ids > i, cols[i] * (1.0 / pivot), 0.0)
            left = left - mult * left[i : i + 1, :]
            right = right - mult * right[i : i + 1, :]
            for j in range(i + 1, 8):
                cols[j] = cols[j] - mult * cols[j][i : i + 1, :]
        done.append(right[:8] * jnp.concatenate(scales, axis=0))
        left = left[8:]
        right = right[8:]
    return jnp.concatenate(done, axis=0)


def dot_nt(a, b):
    return lax.dot_general(a, b, (((1,), (1,)), ((), ())), precision=HI, preferred_element_type=jnp.float32)


def dot_nn(a, b):
    return lax.dot_general(a, b, (((1,), (0,)), ((), ())), precision=HI, preferred_element_type=jnp.float32)


def symmetrise(raw_ref, a_ref):
    for i in range(PW // NB):
        for k in range(i + 1):
            ri, rk = slice(i * NB, (i + 1) * NB), slice(k * NB, (k + 1) * NB)
            a_ref[ri, rk] = (raw_ref[ri, rk] + raw_ref[rk, ri].T) * 0.5


def chol_inverse(a_ref, w_ref, block_done):
    n = a_ref.shape[0]
    steps = n // NB
    w_ref[...] = jnp.zeros_like(w_ref)

    def run(step, carry):
        here = pl.ds(pl.multiple_of(step * NB, NB), NB)
        inv = block_inverse(a_ref[here, here])
        for j in range(steps):

            @pl.when(step == j)
            def _(j=j):
                me = slice(j * NB, (j + 1) * NB)
                w_ref[me, me] = inv
                if j > 0:
                    below = dot_nn(a_ref[me, : j * NB], w_ref[: j * NB, : j * NB])
                    w_ref[me, : j * NB] = -dot_nn(inv, below)
                if j + 1 < steps:
                    rest = slice((j + 1) * NB, n)
                    col = dot_nt(a_ref[rest, me], inv)
                    a_ref[rest, me] = col
                    for k in range(j + 1, steps):
                        low = col[(k - j - 1) * NB :]
                        a_ref[k * NB :, k * NB : (k + 1) * NB] -= dot_nt(low, low[:NB])

        block_done(step)
        return carry

    lax.fori_loop(0, steps, run, 0)


def pack_kernel(dest_ref, tiles_ref, out_ref, target_ref, count_ref, sems):
    def clear_count(i, carry):
        count_ref[i] = 0
        return carry

    def clear_target(i, carry):
        target_ref[i] = -1
        return carry

    lax.fori_loop(0, ROWS, clear_count, 0)
    lax.fori_loop(0, SLOTS, clear_target, 0)
    count = tiles_ref.shape[0]

    def place(i, carry):
        tile = dest_ref[i]
        tile_row = tile >> 6
        owner = tile_row >> 2
        rank = count_ref[owner]
        count_ref[owner] = rank + 1
        slot = owner * CAP + rank
        target_ref[slot] = (tile_row & 3) * 8 + (tile & 7)
        pltpu.make_async_copy(tiles_ref.at[i], out_ref.at[slot], sems.at[i]).start()
        return carry

    def finish(i, carry):
        pltpu.make_async_copy(tiles_ref.at[i], out_ref.at[i], sems.at[i]).wait()
        return carry

    lax.fori_loop(0, count, place, 0)
    lax.fori_loop(0, count, finish, 0)


def pack(child_tiles, child_dest):
    count = child_tiles.shape[0]
    return pl.pallas_call(
        pack_kernel,
        out_shape=(
            jax.ShapeDtypeStruct((SLOTS, TW, TW), jnp.bfloat16),
            jax.ShapeDtypeStruct((SLOTS,), jnp.int32),
        ),
        in_specs=[pl.BlockSpec(memory_space=pltpu.SMEM), pl.BlockSpec(memory_space=pltpu.VMEM)],
        out_specs=(ANY, pl.BlockSpec(memory_space=pltpu.SMEM)),
        scratch_shapes=[pltpu.SMEM((ROWS,), jnp.int32), pltpu.SemaphoreType.DMA((count,))],
        compiler_params=pltpu.CompilerParams(vmem_limit_bytes=58 * MIB),
        name="pack",
    )(child_dest, child_tiles)


PEERS = (
    (2, 1, 0), (2, 1, 1), (1, 1, 0), (1, 1, 1), (2, 0, 0), (2, 0, 1), (3, 1, 0), (3, 1, 1),
    (0, 1, 0), (0, 1, 1), (1, 0, 0), (1, 0, 1), (3, 0, 0), (3, 0, 1), (0, 0, 1),
)


def exchange_kernel(out_ref, target_ref, in_ref, place_ref, send, recv, target_send, target_recv, local):
    r = lax.axis_index("row")
    c = lax.axis_index("col")
    x, y, k = r // 4, (r // 2) % 2, r % 2
    here = pl.ds(r * CAP, CAP)
    copies = []
    for i, (dx, dy, dk) in enumerate(PEERS):
        peer = lax.rem(x + dx, 4) * 4 + lax.rem(y + dy, 2) * 2 + lax.rem(k + dk, 2)
        copies.append(
            pltpu.make_async_remote_copy(
                target_ref.at[peer], place_ref.at[r], target_send.at[i], target_recv.at[i],
                device_id=(peer, c), device_id_type=MESH,
            )
        )
        copies.append(
            pltpu.make_async_remote_copy(
                out_ref.at[pl.ds(peer * CAP, CAP)], in_ref.at[here], send.at[i], recv.at[i],
                device_id=(peer, c), device_id_type=MESH,
            )
        )
    copies.append(pltpu.make_async_copy(out_ref.at[here], in_ref.at[here], local.at[0]))
    copies.append(pltpu.make_async_copy(target_ref.at[r], place_ref.at[r], local.at[1]))
    for copy in copies:
        copy.start()
    for copy in copies:
        copy.wait()


def exchange(outgoing, targets):
    dma = pltpu.SemaphoreType.DMA
    padded = jnp.pad(targets.reshape(ROWS, 1, CAP), ((0, 0), (0, 7), (0, 128 - CAP)))
    arrived, places = pl.pallas_call(
        exchange_kernel,
        out_shape=(
            jax.ShapeDtypeStruct(outgoing.shape, outgoing.dtype),
            jax.ShapeDtypeStruct(padded.shape, padded.dtype),
        ),
        in_specs=[ANY, ANY],
        out_specs=(ANY, ANY),
        scratch_shapes=[dma((15,)), dma((15,)), dma((15,)), dma((15,)), dma((2,))],
        compiler_params=pltpu.CompilerParams(has_side_effects=True),
        name="exchange",
    )(outgoing, padded)
    return arrived, places[:, 0, :CAP].reshape(SLOTS)


def build_lists(places_ref, head_ref, next_ref):
    def clear(i, carry):
        head_ref[i] = -1
        return carry

    lax.fori_loop(0, 32, clear, 0)

    def link(i, carry):
        slot = SLOTS - 1 - i
        tile = places_ref[slot]

        @pl.when(tile >= 0)
        def _():
            next_ref[slot] = head_ref[tile]
            head_ref[tile] = slot

        return carry

    lax.fori_loop(0, SLOTS, link, 0)


def walk(tile, head_ref, next_ref, visit):
    def more(slot):
        return slot >= 0

    def step(slot):
        visit(slot)
        return next_ref[slot]

    lax.while_loop(more, step, head_ref[tile])


def fetch(arrived_ref, tiles_ref, sems, slot):
    return pltpu.make_async_copy(arrived_ref.at[slot], tiles_ref.at[slot], sems.at[slot])


def fetch_tiles(tiles, arrived_ref, tiles_ref, sems, head_ref, next_ref):
    for tile in tiles:
        walk(tile, head_ref, next_ref, lambda slot: fetch(arrived_ref, tiles_ref, sems, slot).start())


def add_children(tile, total_ref, arrived_ref, tiles_ref, sems, head_ref, next_ref):
    def add(slot):
        fetch(arrived_ref, tiles_ref, sems, slot).wait()
        total_ref[...] += tiles_ref[slot].astype(jnp.float32)

    walk(tile, head_ref, next_ref, add)


def panel_kernel(places_ref, front_ref, arrived_ref, out_ref, tiles_ref, sems, head_ref, next_ref):
    step = pl.program_id(0)

    @pl.when(step == 0)
    def _():
        build_lists(places_ref, head_ref, next_ref)
        tiles = [8 * i + j for i in range(4) for j in range(PW // TW)]
        fetch_tiles(tiles, arrived_ref, tiles_ref, sems, head_ref, next_ref)

    out_ref[...] = front_ref[...]
    for j in range(PW // TW):
        total = out_ref.at[:, j * TW : (j + 1) * TW]
        add_children(step * 8 + j, total, arrived_ref, tiles_ref, sems, head_ref, next_ref)


def panel_sum(places, front_init, arrived):
    return pl.pallas_call(
        panel_kernel,
        grid=(front_init.shape[0] // TW,),
        out_shape=jax.ShapeDtypeStruct((front_init.shape[0], PW), jnp.float32),
        in_specs=[
            pl.BlockSpec(memory_space=pltpu.SMEM),
            pl.BlockSpec((TW, PW), lambda i: (i, 0)),
            ANY,
        ],
        out_specs=pl.BlockSpec((TW, PW), lambda i: (i, 0)),
        scratch_shapes=[
            pltpu.VMEM((SLOTS, TW, TW), jnp.bfloat16),
            pltpu.SemaphoreType.DMA((SLOTS,)),
            pltpu.SMEM((32,), jnp.int32),
            pltpu.SMEM((SLOTS,), jnp.int32),
        ],
        compiler_params=pltpu.CompilerParams(vmem_limit_bytes=58 * MIB),
        name="panel_sum",
    )(places, front_init, arrived)


PARTS = 8
LAG = 1
SUB = 128 // PARTS
UPWARD = (1, 5, 2, 0)
DOWNWARD = (3, 7, 6, 4)
CHIPS = ((2, 1), (1, 1), (3, 1), (2, 0), (0, 1), (1, 0), (3, 0))


def spread_kernel(
    p_ref, prs_ref, wa_ref, a_ref, w_ref,
    s_flow, r_flow, s_swap, r_swap, s_pry, r_pry, s_pr3, r_pr3, s_ps2, r_ps2, s_ps3, r_ps3,
    s_w1, r_w1, s_w2, r_w2, s_w3, r_w3, s_w4, r_w4, local,
):
    r = lax.axis_index("row")
    c = lax.axis_index("col")
    m, k = r // 2, r % 2
    x, y = m // 2, m % 2
    yh, z = c // 4, c % 4
    root = (r == 0) & (c == 0)
    other_core = (2 * m + 1 - k, c)

    def remote(src, dst, send, recv, dev):
        return pltpu.make_async_remote_copy(src, dst, send, recv, device_id=dev, device_id_type=MESH)

    def rows(start, size):
        return pl.ds(pl.multiple_of(start, 8), size)

    def each(lo, hi, fn):
        def step(i, carry):
            fn(i)
            return carry

        lax.fori_loop(lo, hi, step, 0)

    to_m = [m] + [lax.rem(x + dx, 4) * 2 + lax.rem(y + dy, 2) for dx, dy in CHIPS]
    from_m = [m] + [lax.rem(x + 4 - dx, 4) * 2 + lax.rem(y + dy, 2) for dx, dy in CHIPS]

    def piece_at(position):
        px, py = position // 2, position % 2
        turn = lax.rem(px + 4 - c // 2, 4)
        return (turn // 2) * 4 + lax.rem(turn, 2) * 2 + lax.rem(py + 2 - c % 2, 2)

    def part_of(piece, ch):
        return rows(128 * piece + SUB * ch, SUB)

    def flow(ch, piece, src):
        part = part_of(piece, ch)
        there = lax.rem(z + (1 if piece in UPWARD else 3), 4)
        i = ch * 8 + piece
        return remote(src.at[part], prs_ref.at[part], s_flow.at[i], r_flow.at[i], (r, there))

    def pry(ch, half):
        part = part_of(z + 4 * half, ch)
        j = ch * 2 + half
        return remote(prs_ref.at[part], prs_ref.at[part], s_pry.at[j], r_pry.at[j], (r, z + 4))

    def pr3(ch, dz, half):
        part = part_of(z + 4 * half, ch)
        i = ch * 6 + (dz - 1) * 2 + half
        return remote(
            prs_ref.at[part], prs_ref.at[part], s_pr3.at[i], r_pr3.at[i], (r, yh * 4 + lax.rem(z + dz, 4))
        )

    def swap(ch):
        there = rows(PW + PW * k + 128 * c + SUB * ch, SUB)
        spot = lax.rem(yh * 2 + z // 2 + x, 4) * 2 + lax.rem(z + y, 2)
        return remote(prs_ref.at[part_of(c, ch)], prs_ref.at[there], s_swap.at[ch], r_swap.at[ch], (2 * spot + k, m))

    def ps_rows(ch, o):
        return rows(PW + PW * k + 128 * piece_at(from_m[o]) + SUB * ch, SUB)

    def ps2(ch, o):
        part = ps_rows(ch, 0)
        i = ch * 8 + o
        return remote(prs_ref.at[part], prs_ref.at[part], s_ps2.at[i], r_ps2.at[i], (2 * to_m[o] + k, c))

    def ps3(ch, o):
        part = ps_rows(ch, o)
        i = ch * 8 + o
        return remote(prs_ref.at[part], prs_ref.at[part], s_ps3.at[i], r_ps3.at[i], other_core)

    def w1(q):
        part = rows(8 * q, 8)
        return remote(w_ref.at[part], wa_ref.at[part], s_w1.at[q], r_w1.at[0], (q // 8, q % 8))

    def w2(o):
        part = rows(8 * (r * 8 + c), 8)
        return remote(wa_ref.at[part], wa_ref.at[part], s_w2.at[o], r_w2.at[o], (r, lax.rem(c + o, 8)))

    def w_rows(o):
        return rows(64 * (2 * from_m[o] + k), 64)

    halves = (pl.ds(0, PW // 2), pl.ds(PW // 2, PW // 2))

    def w3(o, half):
        part = wa_ref.at[w_rows(0), halves[half]]
        i = half * 8 + o
        return remote(part, part, s_w3.at[i], r_w3.at[i], (2 * to_m[o] + k, c))

    def w4(o, half):
        part = wa_ref.at[w_rows(o), halves[half]]
        i = half * 8 + o
        return remote(part, part, s_w4.at[i], r_w4.at[i], other_core)

    def move(src, dst, sem):
        copy = pltpu.make_async_copy(src, dst, sem)
        copy.start()
        copy.wait()

    stays = (m == 0) & (c == 0)

    def send_parts(ch):
        for up, down in zip(UPWARD, DOWNWARD):
            flow(ch, up, p_ref).start()
            flow(ch, down, p_ref).start()

    @pl.when(c == 0)
    def _():
        send_parts(0)
        move(p_ref, w_ref, local.at[0])
        move(w_ref, prs_ref.at[pl.ds(0, PW)], local.at[1])

        @pl.when(m == 0)
        def _():
            move(w_ref.at[pl.ds(0, 128)], prs_ref.at[rows(PW + PW * k, 128)], local.at[2])

    rises = (yh == 0) & ((z == 1) | (z == 2))
    falls = (yh == 0) & ((z == 2) | (z == 3))

    def forward(ch, pieces):
        for piece in pieces:
            flow(ch, piece, prs_ref).wait_recv()
            flow(ch, piece, prs_ref).start()

    def take(ch):
        @pl.when((c == 0) & (ch > 0))
        def _():
            send_parts(ch)

        @pl.when(rises)
        def _():
            forward(ch, UPWARD)

        @pl.when(falls)
        def _():
            forward(ch, DOWNWARD)

        @pl.when(yh == 0)
        def _():
            for half in (1, 0):
                pry(ch, half).start()

        @pl.when(yh == 1)
        def _():
            for half in (1, 0):
                pry(ch, half).wait_recv()

        @pl.when(jnp.logical_not(stays))
        def _():
            swap(ch).start()

        @pl.when(yh == 1)
        def _():
            for dz in (2, 1, 3):
                for half in (0, 1):
                    pr3(ch, dz, half).start()

    def fan(ch):
        @pl.when(jnp.logical_not(stays))
        def _():
            swap(ch).wait_recv()

        for o in range(1, 8):
            ps2(ch, o).start()
        ps3(ch, 0).start()

    def pipeline(i):
        @pl.when(i < PARTS)
        def _():
            take(i)

        @pl.when(i >= LAG)
        def _():
            fan(i - LAG)

    each(0, PARTS, pipeline)

    def send_block(step):
        def send(i):
            q = step * 16 + i

            @pl.when(q > 0)
            def _():
                w1(q).start()

        each(0, 16, send)

    @pl.when(root)
    def _():
        symmetrise(w_ref, a_ref)
        chol_inverse(a_ref, w_ref, send_block)
        move(w_ref.at[pl.ds(0, 8)], wa_ref.at[pl.ds(0, 8)], local.at[2])

    @pl.when(jnp.logical_not(root))
    def _():
        w1(0).wait_recv()

    each(1, 8, lambda o: w2(o).start())
    each(1, 8, lambda o: w2(o).wait_recv())
    for o in range(1, 8):
        w3(o, 0).start()
    w4(0, 0).start()

    @pl.when(m >= 4)
    def _():
        for o in range(1, 8):
            w3(o, 1).start()
        w4(0, 1).start()

    each(PARTS, PARTS + LAG, pipeline)

    def cross(ch):
        for o in range(1, 8):
            ps2(ch, o).wait_recv()
            ps3(ch, o).start()

    each(0, PARTS, cross)
    for o in range(1, 8):
        w3(o, 0).wait_recv()
        w4(o, 0).start()

        @pl.when(from_m[o] >= 4)
        def _(o=o):
            w3(o, 1).wait_recv()
            w4(o, 1).start()


    @pl.when(root)
    def _():
        each(1, ROWS * COLS, lambda q: w1(q).wait_send())

    def finish(ch):
        def settle(pieces, done):
            for piece in pieces:
                copy = flow(ch, piece, prs_ref)
                copy.wait_send() if done else copy.wait_recv()

        @pl.when(rises | (c == 0))
        def _():
            settle(UPWARD, True)

        @pl.when(falls | (c == 0))
        def _():
            settle(DOWNWARD, True)

        @pl.when((yh == 0) & (z == 1))
        def _():
            settle(DOWNWARD, False)

        @pl.when((yh == 0) & (z == 3))
        def _():
            settle(UPWARD, False)

        @pl.when(yh == 0)
        def _():
            for half in (0, 1):
                pry(ch, half).wait_send()

        @pl.when(jnp.logical_not(stays))
        def _():
            swap(ch).wait_send()

        @pl.when(yh == 1)
        def _():
            for dz in (1, 2, 3):
                for half in (0, 1):
                    pr3(ch, dz, half).wait()

        for o in range(1, 8):
            ps2(ch, o).wait_send()
        for o in range(8):
            ps3(ch, o).wait()

    each(0, PARTS, finish)
    for o in range(1, 8):
        w2(o).wait_send()
        w3(o, 0).wait_send()
    for o in range(8):
        w4(o, 0).wait()

        @pl.when(from_m[o] >= 4)
        def _(o=o):
            w4(o, 1).wait()

    @pl.when(m >= 4)
    def _():
        for o in range(1, 8):
            w3(o, 1).wait_send()


def spread(panel):
    dma = pltpu.SemaphoreType.DMA
    n = PARTS
    sizes = [8 * n, 8 * n, n, n, 2 * n, 2 * n, 6 * n, 6 * n, 8 * n, 8 * n, 8 * n, 8 * n, 128, 1, 8, 8, 16, 16, 16, 16, 3]
    return pl.pallas_call(
        spread_kernel,
        out_shape=(
            jax.ShapeDtypeStruct((3 * PW, PW), jnp.float32),
            jax.ShapeDtypeStruct((PW, PW), jnp.float32),
        ),
        in_specs=[ANY],
        out_specs=(ANY, ANY),
        scratch_shapes=[
            pltpu.VMEM((PW, PW), jnp.float32),
            pltpu.VMEM((PW, PW), jnp.float32),
        ]
        + [dma((size,)) for size in sizes],
        compiler_params=pltpu.CompilerParams(has_side_effects=True, vmem_limit_bytes=58 * MIB),
        name="spread",
    )(panel)


def split(x):
    high = x.astype(jnp.bfloat16)
    return high, (x - high.astype(jnp.float32)).astype(jnp.bfloat16)


def dot3(ah, al, bh, bl):
    def nt(a, b):
        return lax.dot_general(a, b, (((1,), (1,)), ((), ())), preferred_element_type=jnp.float32)

    return nt(ah, bh) + (nt(ah, bl) + nt(al, bh))


CHUNK = 512
WIDE = 512
FILL = 3 * PW // CHUNK


def update_kernel(
    places_ref, w_ref, prs_ref, front_ref, arrived_ref, factor_ref, schur_ref,
    wh_ref, wl_ref, fh_ref, fl_ref, tiles_ref, sems, head_ref, next_ref,
):
    step = pl.program_id(0)

    @pl.when(step == 0)
    def _():
        build_lists(places_ref, head_ref, next_ref)
        fetch_tiles(range(32), arrived_ref, tiles_ref, sems, head_ref, next_ref)
        wh_ref[...], wl_ref[...] = split(w_ref[...])

    @pl.when(step < FILL)
    def _():
        ah, al = split(prs_ref[...])
        here = pl.ds(pl.multiple_of(step * CHUNK, CHUNK), CHUNK)
        for j in range(PW // WIDE):
            out = slice(j * WIDE, (j + 1) * WIDE)
            deep = slice(0, (j + 1) * WIDE)
            block = dot3(ah[:, deep], al[:, deep], wh_ref[out, deep], wl_ref[out, deep])
            fh_ref[here, out], fl_ref[here, out] = split(block)

            @pl.when(step < PW // CHUNK)
            def _():
                factor_ref[:, out] = block

    @pl.when(step >= FILL)
    def _():
        column = step - FILL
        right = pl.ds(pl.multiple_of(PW + column * TW, TW), TW)
        schur_ref[...] = front_ref[...] - dot3(fh_ref[:PW, :], fl_ref[:PW, :], fh_ref[right, :], fl_ref[right, :])
        for i in range(PW // TW):
            total = schur_ref.at[i * TW : (i + 1) * TW, :]
            add_children(i * 8 + column, total, arrived_ref, tiles_ref, sems, head_ref, next_ref)


def update(places, inverse, strips, front_init, arrived):
    def column_map(i):
        return (0, jnp.maximum(i - FILL, 0))

    return pl.pallas_call(
        update_kernel,
        grid=(FILL + 8,),
        out_shape=(
            jax.ShapeDtypeStruct((PW, PW), jnp.float32),
            jax.ShapeDtypeStruct(front_init.shape, jnp.float32),
        ),
        in_specs=[
            pl.BlockSpec(memory_space=pltpu.SMEM),
            pl.BlockSpec((PW, PW), lambda i: (0, 0), pipeline_mode=pl.Buffered(1)),
            pl.BlockSpec((CHUNK, PW), lambda i: (jnp.minimum(i, FILL - 1), 0)),
            pl.BlockSpec((PW, TW), column_map),
            ANY,
        ],
        out_specs=(
            pl.BlockSpec((CHUNK, PW), lambda i: (jnp.minimum(i, PW // CHUNK - 1), 0)),
            pl.BlockSpec((PW, TW), column_map),
        ),
        scratch_shapes=[
            pltpu.VMEM((PW, PW), jnp.bfloat16),
            pltpu.VMEM((PW, PW), jnp.bfloat16),
            pltpu.VMEM((3 * PW, PW), jnp.bfloat16),
            pltpu.VMEM((3 * PW, PW), jnp.bfloat16),
            pltpu.VMEM((SLOTS, TW, TW), jnp.bfloat16),
            pltpu.SemaphoreType.DMA((SLOTS,)),
            pltpu.SMEM((32,), jnp.int32),
            pltpu.SMEM((SLOTS,), jnp.int32),
        ],
        compiler_params=pltpu.CompilerParams(vmem_limit_bytes=58 * MIB),
        name="update",
    )(places, inverse, strips, front_init, arrived)


def body(front_init, child_tiles, child_dest):
    outgoing, targets = pack(child_tiles, child_dest)
    arrived, places = exchange(outgoing, targets)
    panel = panel_sum(places, front_init, arrived)
    strips, inverse = spread(panel)
    return update(places, inverse, strips, front_init, arrived)


def solution(mesh):
    return jax.shard_map(
        body,
        mesh=mesh,
        in_specs=(P("row", "col"), P(("row", "col"), None, None), P(("row", "col"))),
        out_specs=(P("row", None), P("row", "col")),
        check_vma=False,
    )
```

```python
import jax
import jax.numpy as jnp
from jax import lax
from jax.experimental import pallas as pl
from jax.experimental.pallas import tpu as pltpu
from jax.sharding import PartitionSpec as P

PW = 1024
TW = 256
CAP = 4
NT = 64
ROWS = 16
COLS = 8
SLOTS = ROWS * CAP
MIB = 1024 * 1024
MESH = pl.DeviceIdType.MESH
ANY = pl.BlockSpec(memory_space=pl.ANY)

HI = lax.Precision.HIGHEST
NB = 128


def block_inverse(block):
    rows = lax.broadcasted_iota(jnp.int32, (NB, NB), 0)
    lanes = lax.broadcasted_iota(jnp.int32, (NB, NB), 1)
    left = block
    right = jnp.where(rows == lanes, 1.0, 0.0).astype(jnp.float32)
    done = []
    for group in range(NB // 8):
        height = NB - 8 * group
        row_ids = lax.broadcasted_iota(jnp.int32, (height, NB), 0)
        cols = [
            jnp.broadcast_to(left[:, 8 * group + j : 8 * group + j + 1], (height, NB))
            for j in range(8)
        ]
        scales = []
        for i in range(8):
            pivot = cols[i][i : i + 1, :]
            scales.append(lax.rsqrt(pivot))
            mult = jnp.where(row_ids > i, cols[i] * (1.0 / pivot), 0.0)
            left = left - mult * left[i : i + 1, :]
            right = right - mult * right[i : i + 1, :]
            for j in range(i + 1, 8):
                cols[j] = cols[j] - mult * cols[j][i : i + 1, :]
        done.append(right[:8] * jnp.concatenate(scales, axis=0))
        left = left[8:]
        right = right[8:]
    return jnp.concatenate(done, axis=0)


def dot_nt(a, b):
    return lax.dot_general(a, b, (((1,), (1,)), ((), ())), precision=HI, preferred_element_type=jnp.float32)


def dot_nn(a, b):
    return lax.dot_general(a, b, (((1,), (0,)), ((), ())), precision=HI, preferred_element_type=jnp.float32)


def symmetrise(raw_ref, a_ref):
    for i in range(PW // NB):
        for k in range(i + 1):
            ri, rk = slice(i * NB, (i + 1) * NB), slice(k * NB, (k + 1) * NB)
            a_ref[ri, rk] = (raw_ref[ri, rk] + raw_ref[rk, ri].T) * 0.5


def chol_inverse(a_ref, w_ref, block_done):
    n = a_ref.shape[0]
    steps = n // NB
    w_ref[...] = jnp.zeros_like(w_ref)

    def run(step, carry):
        here = pl.ds(pl.multiple_of(step * NB, NB), NB)
        inv = block_inverse(a_ref[here, here])
        for j in range(steps):

            @pl.when(step == j)
            def _(j=j):
                me = slice(j * NB, (j + 1) * NB)
                w_ref[me, me] = inv
                if j > 0:
                    below = dot_nn(a_ref[me, : j * NB], w_ref[: j * NB, : j * NB])
                    w_ref[me, : j * NB] = -dot_nn(inv, below)
                if j + 1 < steps:
                    rest = slice((j + 1) * NB, n)
                    col = dot_nt(a_ref[rest, me], inv)
                    a_ref[rest, me] = col
                    for k in range(j + 1, steps):
                        low = col[(k - j - 1) * NB :]
                        a_ref[k * NB :, k * NB : (k + 1) * NB] -= dot_nt(low, low[:NB])

        block_done(step)
        return carry

    lax.fori_loop(0, steps, run, 0)


def pack_kernel(dest_ref, tiles_ref, out_ref, target_ref, count_ref, sems):
    def clear_count(i, carry):
        count_ref[i] = 0
        return carry

    def clear_target(i, carry):
        target_ref[i] = -1
        return carry

    lax.fori_loop(0, ROWS, clear_count, 0)
    lax.fori_loop(0, SLOTS, clear_target, 0)
    count = tiles_ref.shape[0]

    def place(i, carry):
        tile = dest_ref[i]
        tile_row = tile >> 6
        owner = tile_row >> 2
        rank = count_ref[owner]
        count_ref[owner] = rank + 1
        slot = owner * CAP + rank
        target_ref[slot] = (tile_row & 3) * 8 + (tile & 7)
        pltpu.make_async_copy(tiles_ref.at[i], out_ref.at[slot], sems.at[i]).start()
        return carry

    def finish(i, carry):
        pltpu.make_async_copy(tiles_ref.at[i], out_ref.at[i], sems.at[i]).wait()
        return carry

    lax.fori_loop(0, count, place, 0)
    lax.fori_loop(0, count, finish, 0)


def pack(child_tiles, child_dest):
    count = child_tiles.shape[0]
    return pl.pallas_call(
        pack_kernel,
        out_shape=(
            jax.ShapeDtypeStruct((SLOTS, TW, TW), jnp.bfloat16),
            jax.ShapeDtypeStruct((SLOTS,), jnp.int32),
        ),
        in_specs=[pl.BlockSpec(memory_space=pltpu.SMEM), pl.BlockSpec(memory_space=pltpu.VMEM)],
        out_specs=(ANY, pl.BlockSpec(memory_space=pltpu.SMEM)),
        scratch_shapes=[pltpu.SMEM((ROWS,), jnp.int32), pltpu.SemaphoreType.DMA((count,))],
        compiler_params=pltpu.CompilerParams(vmem_limit_bytes=58 * MIB),
        name="pack",
    )(child_dest, child_tiles)


PEERS = (
    (2, 1, 0), (2, 1, 1), (1, 1, 0), (1, 1, 1), (2, 0, 0), (2, 0, 1), (3, 1, 0), (3, 1, 1),
    (0, 1, 0), (0, 1, 1), (1, 0, 0), (1, 0, 1), (3, 0, 0), (3, 0, 1), (0, 0, 1),
)


def exchange_kernel(out_ref, target_ref, in_ref, place_ref, send, recv, target_send, target_recv, local):
    r = lax.axis_index("row")
    c = lax.axis_index("col")
    x, y, k = r // 4, (r // 2) % 2, r % 2
    here = pl.ds(r * CAP, CAP)
    copies = []
    for i, (dx, dy, dk) in enumerate(PEERS):
        peer = lax.rem(x + dx, 4) * 4 + lax.rem(y + dy, 2) * 2 + lax.rem(k + dk, 2)
        copies.append(
            pltpu.make_async_remote_copy(
                target_ref.at[peer], place_ref.at[r], target_send.at[i], target_recv.at[i],
                device_id=(peer, c), device_id_type=MESH,
            )
        )
        copies.append(
            pltpu.make_async_remote_copy(
                out_ref.at[pl.ds(peer * CAP, CAP)], in_ref.at[here], send.at[i], recv.at[i],
                device_id=(peer, c), device_id_type=MESH,
            )
        )
    copies.append(pltpu.make_async_copy(out_ref.at[here], in_ref.at[here], local.at[0]))
    copies.append(pltpu.make_async_copy(target_ref.at[r], place_ref.at[r], local.at[1]))
    for copy in copies:
        copy.start()
    for copy in copies:
        copy.wait()


def exchange(outgoing, targets):
    dma = pltpu.SemaphoreType.DMA
    padded = jnp.pad(targets.reshape(ROWS, 1, CAP), ((0, 0), (0, 7), (0, 128 - CAP)))
    arrived, places = pl.pallas_call(
        exchange_kernel,
        out_shape=(
            jax.ShapeDtypeStruct(outgoing.shape, outgoing.dtype),
            jax.ShapeDtypeStruct(padded.shape, padded.dtype),
        ),
        in_specs=[ANY, ANY],
        out_specs=(ANY, ANY),
        scratch_shapes=[dma((15,)), dma((15,)), dma((15,)), dma((15,)), dma((2,))],
        compiler_params=pltpu.CompilerParams(has_side_effects=True),
        name="exchange",
    )(outgoing, padded)
    return arrived, places[:, 0, :CAP].reshape(SLOTS)


def build_lists(places_ref, head_ref, next_ref):
    def clear(i, carry):
        head_ref[i] = -1
        return carry

    lax.fori_loop(0, 32, clear, 0)

    def link(i, carry):
        slot = SLOTS - 1 - i
        tile = places_ref[slot]

        @pl.when(tile >= 0)
        def _():
            next_ref[slot] = head_ref[tile]
            head_ref[tile] = slot

        return carry

    lax.fori_loop(0, SLOTS, link, 0)


def walk(tile, head_ref, next_ref, visit):
    def more(slot):
        return slot >= 0

    def step(slot):
        visit(slot)
        return next_ref[slot]

    lax.while_loop(more, step, head_ref[tile])


def fetch(arrived_ref, tiles_ref, sems, slot):
    return pltpu.make_async_copy(arrived_ref.at[slot], tiles_ref.at[slot], sems.at[slot])


def fetch_tiles(tiles, arrived_ref, tiles_ref, sems, head_ref, next_ref):
    for tile in tiles:
        walk(tile, head_ref, next_ref, lambda slot: fetch(arrived_ref, tiles_ref, sems, slot).start())


def add_children(tile, total_ref, arrived_ref, tiles_ref, sems, head_ref, next_ref):
    def add(slot):
        fetch(arrived_ref, tiles_ref, sems, slot).wait()
        total_ref[...] += tiles_ref[slot].astype(jnp.float32)

    walk(tile, head_ref, next_ref, add)


def panel_kernel(places_ref, front_ref, arrived_ref, out_ref, tiles_ref, sems, head_ref, next_ref):
    step = pl.program_id(0)

    @pl.when(step == 0)
    def _():
        build_lists(places_ref, head_ref, next_ref)
        tiles = [8 * i + j for i in range(4) for j in range(PW // TW)]
        fetch_tiles(tiles, arrived_ref, tiles_ref, sems, head_ref, next_ref)

    out_ref[...] = front_ref[...]
    for j in range(PW // TW):
        total = out_ref.at[:, j * TW : (j + 1) * TW]
        add_children(step * 8 + j, total, arrived_ref, tiles_ref, sems, head_ref, next_ref)


def panel_sum(places, front_init, arrived):
    return pl.pallas_call(
        panel_kernel,
        grid=(front_init.shape[0] // TW,),
        out_shape=jax.ShapeDtypeStruct((front_init.shape[0], PW), jnp.float32),
        in_specs=[
            pl.BlockSpec(memory_space=pltpu.SMEM),
            pl.BlockSpec((TW, PW), lambda i: (i, 0)),
            ANY,
        ],
        out_specs=pl.BlockSpec((TW, PW), lambda i: (i, 0)),
        scratch_shapes=[
            pltpu.VMEM((SLOTS, TW, TW), jnp.bfloat16),
            pltpu.SemaphoreType.DMA((SLOTS,)),
            pltpu.SMEM((32,), jnp.int32),
            pltpu.SMEM((SLOTS,), jnp.int32),
        ],
        compiler_params=pltpu.CompilerParams(vmem_limit_bytes=58 * MIB),
        name="panel_sum",
    )(places, front_init, arrived)


PARTS = 8
LAG = 1
SUB = 128 // PARTS
UPWARD = (1, 5, 2, 0)
DOWNWARD = (3, 7, 6, 4)
CHIPS = ((2, 1), (1, 1), (3, 1), (2, 0), (0, 1), (1, 0), (3, 0))


def spread_kernel(
    p_ref, prs_ref, wa_ref, a_ref, w_ref,
    s_flow, r_flow, s_swap, r_swap, s_pry, r_pry, s_pr3, r_pr3, s_ps2, r_ps2, s_ps3, r_ps3,
    s_w1, r_w1, s_w2, r_w2, s_w3, r_w3, s_w4, r_w4, local,
):
    r = lax.axis_index("row")
    c = lax.axis_index("col")
    m, k = r // 2, r % 2
    x, y = m // 2, m % 2
    yh, z = c // 4, c % 4
    root = (r == 0) & (c == 0)
    other_core = (2 * m + 1 - k, c)

    def remote(src, dst, send, recv, dev):
        return pltpu.make_async_remote_copy(src, dst, send, recv, device_id=dev, device_id_type=MESH)

    def rows(start, size):
        return pl.ds(pl.multiple_of(start, 8), size)

    def each(lo, hi, fn):
        def step(i, carry):
            fn(i)
            return carry

        lax.fori_loop(lo, hi, step, 0)

    to_m = [m] + [lax.rem(x + dx, 4) * 2 + lax.rem(y + dy, 2) for dx, dy in CHIPS]
    from_m = [m] + [lax.rem(x + 4 - dx, 4) * 2 + lax.rem(y + dy, 2) for dx, dy in CHIPS]

    def piece_at(position):
        px, py = position // 2, position % 2
        turn = lax.rem(px + 4 - c // 2, 4)
        return (turn // 2) * 4 + lax.rem(turn, 2) * 2 + lax.rem(py + 2 - c % 2, 2)

    def part_of(piece, ch):
        return rows(128 * piece + SUB * ch, SUB)

    def flow(ch, piece, src):
        part = part_of(piece, ch)
        there = lax.rem(z + (1 if piece in UPWARD else 3), 4)
        i = ch * 8 + piece
        return remote(src.at[part], prs_ref.at[part], s_flow.at[i], r_flow.at[i], (r, there))

    def pry(ch, half):
        part = part_of(z + 4 * half, ch)
        j = ch * 2 + half
        return remote(prs_ref.at[part], prs_ref.at[part], s_pry.at[j], r_pry.at[j], (r, z + 4))

    def pr3(ch, dz, half):
        part = part_of(z + 4 * half, ch)
        i = ch * 6 + (dz - 1) * 2 + half
        return remote(
            prs_ref.at[part], prs_ref.at[part], s_pr3.at[i], r_pr3.at[i], (r, yh * 4 + lax.rem(z + dz, 4))
        )

    def swap(ch):
        there = rows(PW + PW * k + 128 * c + SUB * ch, SUB)
        spot = lax.rem(yh * 2 + z // 2 + x, 4) * 2 + lax.rem(z + y, 2)
        return remote(prs_ref.at[part_of(c, ch)], prs_ref.at[there], s_swap.at[ch], r_swap.at[ch], (2 * spot + k, m))

    def ps_rows(ch, o):
        return rows(PW + PW * k + 128 * piece_at(from_m[o]) + SUB * ch, SUB)

    def ps2(ch, o):
        part = ps_rows(ch, 0)
        i = ch * 8 + o
        return remote(prs_ref.at[part], prs_ref.at[part], s_ps2.at[i], r_ps2.at[i], (2 * to_m[o] + k, c))

    def ps3(ch, o):
        part = ps_rows(ch, o)
        i = ch * 8 + o
        return remote(prs_ref.at[part], prs_ref.at[part], s_ps3.at[i], r_ps3.at[i], other_core)

    def w1(q):
        part = rows(8 * q, 8)
        return remote(w_ref.at[part], wa_ref.at[part], s_w1.at[q], r_w1.at[0], (q // 8, q % 8))

    def w2(o):
        part = rows(8 * (r * 8 + c), 8)
        return remote(wa_ref.at[part], wa_ref.at[part], s_w2.at[o], r_w2.at[o], (r, lax.rem(c + o, 8)))

    def w_rows(o):
        return rows(64 * (2 * from_m[o] + k), 64)

    halves = (pl.ds(0, PW // 2), pl.ds(PW // 2, PW // 2))

    def w3(o, half):
        part = wa_ref.at[w_rows(0), halves[half]]
        i = half * 8 + o
        return remote(part, part, s_w3.at[i], r_w3.at[i], (2 * to_m[o] + k, c))

    def w4(o, half):
        part = wa_ref.at[w_rows(o), halves[half]]
        i = half * 8 + o
        return remote(part, part, s_w4.at[i], r_w4.at[i], other_core)

    def move(src, dst, sem):
        copy = pltpu.make_async_copy(src, dst, sem)
        copy.start()
        copy.wait()

    stays = (m == 0) & (c == 0)

    def send_parts(ch):
        for up, down in zip(UPWARD, DOWNWARD):
            flow(ch, up, p_ref).start()
            flow(ch, down, p_ref).start()

    @pl.when(c == 0)
    def _():
        send_parts(0)
        move(p_ref, w_ref, local.at[0])
        move(w_ref, prs_ref.at[pl.ds(0, PW)], local.at[1])

        @pl.when(m == 0)
        def _():
            move(w_ref.at[pl.ds(0, 128)], prs_ref.at[rows(PW + PW * k, 128)], local.at[2])

    rises = (yh == 0) & ((z == 1) | (z == 2))
    falls = (yh == 0) & ((z == 2) | (z == 3))

    def forward(ch, pieces):
        for piece in pieces:
            flow(ch, piece, prs_ref).wait_recv()
            flow(ch, piece, prs_ref).start()

    def take(ch):
        @pl.when((c == 0) & (ch > 0))
        def _():
            send_parts(ch)

        @pl.when(rises)
        def _():
            forward(ch, UPWARD)

        @pl.when(falls)
        def _():
            forward(ch, DOWNWARD)

        @pl.when(yh == 0)
        def _():
            for half in (1, 0):
                pry(ch, half).start()

        @pl.when(yh == 1)
        def _():
            for half in (1, 0):
                pry(ch, half).wait_recv()

        @pl.when(jnp.logical_not(stays))
        def _():
            swap(ch).start()

        @pl.when(yh == 1)
        def _():
            for dz in (2, 1, 3):
                for half in (0, 1):
                    pr3(ch, dz, half).start()

    def fan(ch):
        @pl.when(jnp.logical_not(stays))
        def _():
            swap(ch).wait_recv()

        for o in range(1, 8):
            ps2(ch, o).start()
        ps3(ch, 0).start()

    def pipeline(i):
        @pl.when(i < PARTS)
        def _():
            take(i)

        @pl.when(i >= LAG)
        def _():
            fan(i - LAG)

    each(0, PARTS, pipeline)

    def send_block(step):
        def send(i):
            q = step * 16 + i

            @pl.when(q > 0)
            def _():
                w1(q).start()

        each(0, 16, send)

    @pl.when(root)
    def _():
        symmetrise(w_ref, a_ref)
        chol_inverse(a_ref, w_ref, send_block)
        move(w_ref.at[pl.ds(0, 8)], wa_ref.at[pl.ds(0, 8)], local.at[2])

    @pl.when(jnp.logical_not(root))
    def _():
        w1(0).wait_recv()

    each(1, 8, lambda o: w2(o).start())
    each(1, 8, lambda o: w2(o).wait_recv())
    for o in range(1, 8):
        w3(o, 0).start()
    w4(0, 0).start()

    @pl.when(m >= 4)
    def _():
        for o in range(1, 8):
            w3(o, 1).start()
        w4(0, 1).start()

    each(PARTS, PARTS + LAG, pipeline)

    def cross(ch):
        for o in range(1, 8):
            ps2(ch, o).wait_recv()
            ps3(ch, o).start()

    each(0, PARTS, cross)
    for o in range(1, 8):
        w3(o, 0).wait_recv()
        w4(o, 0).start()

        @pl.when(from_m[o] >= 4)
        def _(o=o):
            w3(o, 1).wait_recv()
            w4(o, 1).start()


    @pl.when(root)
    def _():
        each(1, ROWS * COLS, lambda q: w1(q).wait_send())

    def finish(ch):
        def settle(pieces, done):
            for piece in pieces:
                copy = flow(ch, piece, prs_ref)
                copy.wait_send() if done else copy.wait_recv()

        @pl.when(rises | (c == 0))
        def _():
            settle(UPWARD, True)

        @pl.when(falls | (c == 0))
        def _():
            settle(DOWNWARD, True)

        @pl.when((yh == 0) & (z == 1))
        def _():
            settle(DOWNWARD, False)

        @pl.when((yh == 0) & (z == 3))
        def _():
            settle(UPWARD, False)

        @pl.when(yh == 0)
        def _():
            for half in (0, 1):
                pry(ch, half).wait_send()

        @pl.when(jnp.logical_not(stays))
        def _():
            swap(ch).wait_send()

        @pl.when(yh == 1)
        def _():
            for dz in (1, 2, 3):
                for half in (0, 1):
                    pr3(ch, dz, half).wait()

        for o in range(1, 8):
            ps2(ch, o).wait_send()
        for o in range(8):
            ps3(ch, o).wait()

    each(0, PARTS, finish)
    for o in range(1, 8):
        w2(o).wait_send()
        w3(o, 0).wait_send()
    for o in range(8):
        w4(o, 0).wait()

        @pl.when(from_m[o] >= 4)
        def _(o=o):
            w4(o, 1).wait()

    @pl.when(m >= 4)
    def _():
        for o in range(1, 8):
            w3(o, 1).wait_send()


def spread(panel):
    dma = pltpu.SemaphoreType.DMA
    n = PARTS
    sizes = [8 * n, 8 * n, n, n, 2 * n, 2 * n, 6 * n, 6 * n, 8 * n, 8 * n, 8 * n, 8 * n, 128, 1, 8, 8, 16, 16, 16, 16, 3]
    return pl.pallas_call(
        spread_kernel,
        out_shape=(
            jax.ShapeDtypeStruct((3 * PW, PW), jnp.float32),
            jax.ShapeDtypeStruct((PW, PW), jnp.float32),
        ),
        in_specs=[ANY],
        out_specs=(ANY, ANY),
        scratch_shapes=[
            pltpu.VMEM((PW, PW), jnp.float32),
            pltpu.VMEM((PW, PW), jnp.float32),
        ]
        + [dma((size,)) for size in sizes],
        compiler_params=pltpu.CompilerParams(has_side_effects=True, vmem_limit_bytes=58 * MIB),
        name="spread",
    )(panel)


def split(x):
    high = x.astype(jnp.bfloat16)
    return high, (x - high.astype(jnp.float32)).astype(jnp.bfloat16)


def dot3(ah, al, bh, bl):
    def nt(a, b):
        return lax.dot_general(a, b, (((1,), (1,)), ((), ())), preferred_element_type=jnp.float32)

    return nt(ah, bh) + (nt(ah, bl) + nt(al, bh))


CHUNK = 512
WIDE = 512
FILL = 3 * PW // CHUNK


def update_kernel(
    places_ref, w_ref, prs_ref, front_ref, arrived_ref, factor_ref, schur_ref,
    wh_ref, wl_ref, fh_ref, fl_ref, tiles_ref, sems, head_ref, next_ref,
):
    step = pl.program_id(0)

    @pl.when(step == 0)
    def _():
        build_lists(places_ref, head_ref, next_ref)
        fetch_tiles(range(32), arrived_ref, tiles_ref, sems, head_ref, next_ref)
        wh_ref[...], wl_ref[...] = split(w_ref[...])

    @pl.when(step < FILL)
    def _():
        ah, al = split(prs_ref[...])
        here = pl.ds(pl.multiple_of(step * CHUNK, CHUNK), CHUNK)
        for j in range(PW // WIDE):
            out = slice(j * WIDE, (j + 1) * WIDE)
            deep = slice(0, (j + 1) * WIDE)
            block = dot3(ah[:, deep], al[:, deep], wh_ref[out, deep], wl_ref[out, deep])
            fh_ref[here, out], fl_ref[here, out] = split(block)

            @pl.when(step < PW // CHUNK)
            def _():
                factor_ref[:, out] = block

    @pl.when(step >= FILL)
    def _():
        column = step - FILL
        right = pl.ds(pl.multiple_of(PW + column * WIDE, WIDE), WIDE)
        schur_ref[...] = front_ref[...] - dot3(fh_ref[:PW, :], fl_ref[:PW, :], fh_ref[right, :], fl_ref[right, :])
        for i in range(PW // TW):
            for j in range(WIDE // TW):
                total = schur_ref.at[i * TW : (i + 1) * TW, j * TW : (j + 1) * TW]
                tile = i * 8 + column * (WIDE // TW) + j
                add_children(tile, total, arrived_ref, tiles_ref, sems, head_ref, next_ref)


def update(places, inverse, strips, front_init, arrived):
    def column_map(i):
        return (0, jnp.maximum(i - FILL, 0))

    return pl.pallas_call(
        update_kernel,
        grid=(FILL + front_init.shape[1] // WIDE,),
        out_shape=(
            jax.ShapeDtypeStruct((PW, PW), jnp.float32),
            jax.ShapeDtypeStruct(front_init.shape, jnp.float32),
        ),
        in_specs=[
            pl.BlockSpec(memory_space=pltpu.SMEM),
            pl.BlockSpec((PW, PW), lambda i: (0, 0), pipeline_mode=pl.Buffered(1)),
            pl.BlockSpec((CHUNK, PW), lambda i: (jnp.minimum(i, FILL - 1), 0)),
            pl.BlockSpec((PW, WIDE), column_map),
            ANY,
        ],
        out_specs=(
            pl.BlockSpec((CHUNK, PW), lambda i: (jnp.minimum(i, PW // CHUNK - 1), 0)),
            pl.BlockSpec((PW, WIDE), column_map),
        ),
        scratch_shapes=[
            pltpu.VMEM((PW, PW), jnp.bfloat16),
            pltpu.VMEM((PW, PW), jnp.bfloat16),
            pltpu.VMEM((3 * PW, PW), jnp.bfloat16),
            pltpu.VMEM((3 * PW, PW), jnp.bfloat16),
            pltpu.VMEM((SLOTS, TW, TW), jnp.bfloat16),
            pltpu.SemaphoreType.DMA((SLOTS,)),
            pltpu.SMEM((32,), jnp.int32),
            pltpu.SMEM((SLOTS,), jnp.int32),
        ],
        compiler_params=pltpu.CompilerParams(vmem_limit_bytes=58 * MIB),
        name="update",
    )(places, inverse, strips, front_init, arrived)


def body(front_init, child_tiles, child_dest):
    outgoing, targets = pack(child_tiles, child_dest)
    arrived, places = exchange(outgoing, targets)
    panel = panel_sum(places, front_init, arrived)
    strips, inverse = spread(panel)
    return update(places, inverse, strips, front_init, arrived)


def solution(mesh):
    return jax.shard_map(
        body,
        mesh=mesh,
        in_specs=(P("row", "col"), P(("row", "col"), None, None), P(("row", "col"))),
        out_specs=(P("row", None), P("row", "col")),
        check_vma=False,
    )
```
